512 devices in a mesh: rep: 8 (over z), mp: 64 (over y, x, core).
Axes of the slice: x: 4, y: 8, z: 8, core: 2. Of those that a mesh axis runs over, the one named last changes fastest.
Arguments:
- pooled_grad: bfloat16 [65536, 8, 256], P(('rep', 'mp')), may hold values from -6 to 6
- owner_ids: int32 [65536, 8, 2, 1], P(('rep', 'mp')), may hold values from 0 to 63; in each aligned block of 2048 rows (0 to 2047, 2048 to 4095, ..., all dimensions but the last counted through in order) at most 48 rows name the same one
- local_ids: int32 [65536, 8, 2], P(('rep', 'mp')), may hold values from 0 to 1023
- feature_table: int32 [8], replicated, may hold values from 0 to 1
- table_rows: bfloat16 [2, 65536, 256], P(None, 'mp'), may hold values from -6 to 6
- adagrad_state: float32 [2, 65536], P(None, 'mp'), may hold values from 0.01 to 1
Outputs:
- new_tables: bfloat16 [2, 65536, 256], P(None, 'mp')
- new_state: float32 [2, 65536], P(None, 'mp')
The draws below stay inside these ranges and needn't reach their ends.
Inputs may be any that keep to these rules, and one draw needn't show every extreme that they name: `owner_ids`: among the lookups of one device, at most 48 name any one owner, and in every draw some owner is named by exactly 48 of them.
All inputs are finite; a program needn't handle non-finite values.
Results may differ from the reference program's by a relative error of at most 0.0034.
Values may be sent and summed in bfloat16 or wider, within the bound.
No kernel may reach another device: no remote copies, remote signals or barrier semaphores. Data moves between devices by JAX's collectives and lax.ppermute only.
A program may use at most 64 MiB of HBM per device.

```python
import math
import jax
import jax.numpy as jnp
import numpy as np
from jax import lax

EMBED = 256
ROWS_DEV = 1024
TABLES = 2
FEATURES = 8
POOL = 2
LOOK_DEV = 2048
OWNERS = 64
CAP = 48
ROWS = 65536
SAMPLES = 65536
N_REP = 8


def with_ends(entries, own_key, smallest, high):
    longest = entries.shape.index(max(entries.shape))
    spots = []
    for shift in (0, 1):
        where = [jax.random.randint(jax.random.fold_in(own_key, axis), (), 0, length) for axis, length in enumerate(entries.shape)]
        where[longest] = (where[longest] + shift) % entries.shape[longest]
        spots.append(tuple(where))
    return entries.at[spots[0]].set(smallest).at[spots[1]].set(high)


def levels(stream_key, extent, pieces, smallest, top_value):
    loudness, own = 1.0, jax.random.fold_in(stream_key, 6)
    for axis_at, blocks in pieces:
        heights = jnp.exp(jax.random.uniform(jax.random.fold_in(own, axis_at), (blocks,), jnp.float32, smallest / len(pieces), top_value / len(pieces)))
        loudness = loudness * jnp.repeat(heights, extent[axis_at] // blocks).reshape([-1 if axis == axis_at else 1 for axis in range(len(extent))])
    return loudness


def cumulative_ranks(amount, slope):
    loads = [(1 << 20) // math.isqrt(standing ** slope) + 1 for standing in range(1, amount + 1)]
    spread = 1 + sum(loads) // (1 << 30)
    return np.cumsum(np.array([max(1, weight // spread) for weight in loads]))


def ranked(key, shape, count, lean):
    table = cumulative_ranks(count, lean)
    ticket = jax.random.randint(jax.random.fold_in(key, 1), shape, 0, int(table[count - 1]))
    grade = jnp.searchsorted(jnp.asarray(table, jnp.int32), ticket, side="right")
    return jax.random.permutation(jax.random.fold_in(key, 2), count)[grade].astype(jnp.int32)


def routed_block(key, own, number, rows, number_of, top, bound, skew):
    ranking = jax.random.permutation(key, number_of)
    heavy_load, ordinary = portions_of(number_of, rows * top, bound, skew, True), portions_of(number_of, rows * top, bound, skew, False)
    places = jnp.arange(number_of)

    def named(sizes, offset_by):
        used = int((sizes > 0).sum())
        fixed = max(1, used // 4)
        shifted = fixed + (places - fixed + offset_by * (used - fixed)) % max(1, number_of - fixed)
        return jnp.zeros((number_of,), jnp.int32).at[ranking[jnp.where(places < fixed, places, shifted)]].set(jnp.asarray(sizes, jnp.int32))

    sizes = jnp.where(number % 4 == 0, named(heavy_load, number // 4), named(ordinary, number - number // 4 - 1))
    mixed = jax.random.permutation(jax.random.fold_in(own, 3), number_of)
    giver, receiver = mixed[0:number_of // 2 * 2:2], mixed[1:number_of // 2 * 2:2]
    room = jnp.minimum(sizes[giver] - 1, bound - sizes[receiver]) // 2
    room = jnp.where((giver == ranking[0]) | (receiver == ranking[0]) | (sizes[receiver] == 0), 0, jnp.maximum(room, 0))
    shifted = jax.random.randint(jax.random.fold_in(own, 4), (number_of // 2,), 0, 1 << 20) % (room + 1)
    sizes = sizes.at[giver].add(-shifted).at[receiver].add(shifted)
    labels = jnp.searchsorted(jnp.cumsum(sizes), jnp.arange(rows * top), side="right").astype(jnp.int32)
    listing = labels.reshape(top, rows).T
    listing = listing[jax.random.permutation(jax.random.fold_in(own, 1), rows)]
    offset_by = jax.random.randint(jax.random.fold_in(own, 2), (rows, 1), 0, top)
    return jnp.take_along_axis(listing, (jnp.arange(top)[None, :] + offset_by) % top, axis=1)


def portions_of(amount, total, bound, slope, full):
    loads = [(1 << 20) // math.isqrt(standing ** slope) + 1 for standing in range(1, amount + 1)]
    largest = bound if full else min(bound, max(-(-total // amount), total * loads[0] // sum(loads)))
    least = 1 if total - largest >= amount - 1 else 0
    holding, surplus = [largest] + [least] * (amount - 1), total - largest - least * (amount - 1)
    while surplus > 0:
        candidates = [i for i in range(1, amount) if holding[i] < largest] or [i for i in range(1, amount) if holding[i] < bound]
        pool, remaining = sum([loads[i] for i in candidates]), surplus
        for i in candidates:
            addition = min(bound - holding[i], max(1, remaining * loads[i] // pool), surplus)
            holding[i] = holding[i] + addition
            surplus = surplus - addition
    return np.array(holding)


def scatter_about(stream_key, extent, width, most, pieces=(), kind=jnp.bfloat16):
    result = width * jax.random.normal(stream_key, extent, jnp.float32)
    if pieces:
        result = result * levels(stream_key, extent, pieces, -0.22, 0.18)
    return jnp.clip(result, -most, most).astype(kind)


def setup_inputs(seed: int = 0) -> dict:
    keys = jax.random.split(jax.random.key(seed), 7)
    pooled_grad = scatter_about(keys[0], (SAMPLES, FEATURES, EMBED), 1.0, 6.0, ((0, 512),))
    owner_ids_keys = jax.random.split(jax.random.fold_in(keys[1], 1), SAMPLES * FEATURES * POOL // LOOK_DEV)
    owner_ids_turns = jax.random.permutation(jax.random.fold_in(keys[1], 3), SAMPLES * FEATURES * POOL // LOOK_DEV)
    owner_ids = jax.vmap(lambda own, number: routed_block(jax.random.fold_in(keys[1], 2), own, number, LOOK_DEV, OWNERS, 1, CAP, 2))(owner_ids_keys, owner_ids_turns).reshape((SAMPLES, FEATURES, POOL, 1))
    local_ids = with_ends(ranked(keys[2], (SAMPLES, FEATURES, POOL), ROWS_DEV, 2), jax.random.fold_in(keys[2], 3), 0, ROWS_DEV - 1).astype(jnp.int32)
    feature_table = with_ends(jax.random.randint(keys[3], (FEATURES,), 0, TABLES), jax.random.fold_in(keys[3], 1), 0, TABLES - 1).astype(jnp.int32)
    table_rows = scatter_about(keys[4], (TABLES, ROWS, EMBED), 1.0, 6.0, ((1, 64),))
    adagrad_state = jnp.clip(jnp.exp(math.log(1.0) - 4.6051702 * jax.random.uniform(keys[5], (TABLES, ROWS), jnp.float32) ** levels(keys[5], (TABLES, ROWS), ((1, 64),), -0.2, 0.2)), 0.01, 1.0)
    return dict(pooled_grad=pooled_grad, owner_ids=owner_ids, local_ids=local_ids, feature_table=feature_table, table_rows=table_rows, adagrad_state=adagrad_state)


def reference(pooled_grad, owner_ids, local_ids, feature_table, table_rows, adagrad_state):
    rows_all = ROWS_DEV * OWNERS
    per_rep = SAMPLES // N_REP
    grads = pooled_grad.reshape(N_REP, per_rep, FEATURES, EMBED)
    owners = owner_ids.reshape(N_REP, per_rep, FEATURES, POOL)
    locals_all = local_ids.reshape(N_REP, per_rep, FEATURES, POOL)
    base = table_rows.astype(jnp.float32)

    def replica(carry, items):
        grad_r, owner_r, local_r = items
        index = feature_table.astype(jnp.int32)[None, :, None] * rows_all + owner_r * ROWS_DEV + local_r
        data = jnp.broadcast_to(grad_r.astype(jnp.float32)[:, :, None, :], (per_rep, FEATURES, POOL, EMBED))
        row_grad = jax.ops.segment_sum(data.reshape(-1, EMBED), index.reshape(-1).astype(jnp.int32), num_segments=TABLES * rows_all)
        row_grad = row_grad.reshape(TABLES, rows_all, EMBED)
        state = adagrad_state + lax.optimization_barrier(jnp.mean(row_grad * row_grad, axis=2))
        updated = (base - 0.3 * row_grad / jnp.sqrt(state)[:, :, None]).astype(jnp.bfloat16)
        updated = lax.optimization_barrier(updated).astype(jnp.float32)
        return ((carry[0] + updated, carry[1] + state), None)
    start = (jnp.zeros((TABLES, rows_all, EMBED), jnp.float32), jnp.zeros((TABLES, rows_all), jnp.float32))
    (table_sum, state_sum), unused = lax.scan(replica, start, (grads, owners, locals_all))
    return ((table_sum / N_REP).astype(jnp.bfloat16), state_sum / N_REP)
```

```python
import jax
import jax.numpy as jnp
from jax import lax
from jax.experimental import pallas as pl
from jax.experimental.pallas import tpu as pltpu
from jax.sharding import PartitionSpec as P

BF = jnp.bfloat16
F32 = jnp.float32
LANES = 128
IDS = 8


def iota(shape, dim):
    return lax.broadcasted_iota(jnp.int32, shape, dim)


def split3(x):
    hi = x.astype(BF).astype(F32)
    mid = (x - hi).astype(BF).astype(F32)
    return hi, mid, x - hi - mid


def pack_kernel(owners, cap, rows_dev, mine, tables_ref, owner_ref, local_ref, grad_ref, out_ref):
    lists, samples = owner_ref.shape
    features = tables_ref.shape[0]
    pool = lists // features
    count = grad_ref.shape[0]
    owner = owner_ref[...]
    table = jnp.zeros((lists, samples), jnp.int32)
    for f in range(features):
        table = jnp.where(iota((lists, samples), 0) // pool == f, tables_ref[f], table)
    target = table * rows_dev + local_ref[...]

    low = iota((samples, 2 * samples), 0)
    col = iota((samples, 2 * samples), 1)
    tri = jnp.where((low <= col), 1.0, 0.0).astype(BF)
    hot = [iota((owners, samples), 0) == owner[r : r + 1, :] for r in range(lists)]
    stacked = jnp.concatenate([jnp.where(h, 1.0, 0.0) for h in hot], axis=0).astype(BF)
    counts = jnp.dot(stacked, tri, preferred_element_type=F32)
    carry = jnp.zeros((owners, samples), F32)
    places = []
    for r in range(lists):
        block = counts[r * owners : (r + 1) * owners]
        running = block[:, :samples] + carry
        places.append(jnp.sum(jnp.where(hot[r], running, 0.0), axis=0, keepdims=True) - 1.0)
        carry = carry + block[:, samples:]
    place = jnp.concatenate(places, axis=0)

    spread = (iota((samples, count), 1) // features == iota((samples, count), 0))
    spread = jnp.where(spread, 1.0, 0.0).astype(BF)
    both = jnp.concatenate([owner.astype(F32), place], axis=0).astype(BF)
    wide = jnp.dot(both, spread, preferred_element_type=F32)
    slots = []
    lane_f = iota((lists, count), 1) % features
    for p in range(pool):
        keep = iota((lists, count), 0) == lane_f * pool + p
        slot = wide[:lists] * cap + wide[lists:]
        slots.append(jnp.sum(jnp.where(keep, slot, 0.0), axis=0, keepdims=True).astype(jnp.int32))

    grad = grad_ref[...]
    group = 8
    for g in range(owners // group):
        rows = group * cap
        index = iota((rows, count), 0) + g * rows
        chosen = index == slots[0]
        for p in range(1, pool):
            chosen = chosen | (index == slots[p])
        picked = jnp.dot(jnp.where(chosen, 1.0, 0.0).astype(BF), grad, preferred_element_type=F32)
        picked = picked.astype(BF)
        for k in range(group):
            part = picked[k * cap : (k + 1) * cap]
            out_ref[g * group + k, 0:cap, :] = part[:, :LANES]
            out_ref[g * group + k, cap : 2 * cap, :] = part[:, LANES:]

    shift = (lax.axis_index("mp") % 8) * cap
    lane = place.astype(jnp.int32) + shift
    chunk = lane // LANES
    low_id = (target % 64).astype(F32)
    high_id = (target // 64).astype(F32)
    left, right = [], []
    kind = iota((IDS, samples), 0)
    for r in range(lists):
        row = slice(r, r + 1)
        value = jnp.where(kind < 3, low_id[row], high_id[row])
        value = jnp.where((kind % 3 == chunk[row]) & (kind < 6), value, 0.0)
        blocks = [jnp.where(owner[row] == o, value, 0.0) for o in range(owners)]
        left.append(jnp.concatenate(blocks, axis=0).astype(BF))
        right.append(jnp.where(lane[row] % LANES == iota((LANES, samples), 0), 1.0, 0.0).astype(BF))
    ids = lax.dot_general(
        jnp.concatenate(left, axis=1),
        jnp.concatenate(right, axis=1),
        (((1,), (1,)), ((), ())),
        preferred_element_type=F32,
    )
    out_ref[:, 2 * cap : 2 * cap + IDS, :] = ids.reshape(owners, IDS, LANES).astype(BF)


def update_kernel(cap, shards, recv_ref, table_ref, state_ref, out_ref):
    senders = recv_ref.shape[0]
    rows = table_ref.shape[0]
    part = rows // shards
    ids = recv_ref[:, 2 * cap : 2 * cap + IDS, :].astype(F32)
    ids = jnp.sum(ids.reshape(senders // 8, 8, IDS, LANES), axis=1)
    group = 16
    where, data = [], []
    for g in range(senders // group):
        lanes = []
        for h in range(group // 8):
            x = ids[g * (group // 8) + h]
            lanes += [x[j : j + 1] + 64.0 * x[j + 3 : j + 4] for j in range(3)]
        where.append(jnp.concatenate(lanes, axis=1).astype(jnp.int32))
        block = recv_ref[g * group : (g + 1) * group, 0 : 2 * cap, :]
        halves = [
            block[:, h * cap : (h + 1) * cap, :].reshape(group * cap, LANES) for h in range(2)
        ]
        data.append(jnp.concatenate(halves, axis=1))
    state = jnp.transpose(state_ref[...])
    for k in range(shards):
        total = jnp.zeros((part, 2 * LANES), F32)
        for g in range(senders // group):
            hot = iota((part, group * cap), 0) + k * part == where[g]
            hot = jnp.where(hot, 1.0, 0.0).astype(BF)
            total = total + jnp.dot(hot, data[g], preferred_element_type=F32)
        square = jnp.sum(total * total, axis=1, keepdims=True) * (1.0 / (2 * LANES))
        columns = []
        for b in range(part // LANES):
            at = k * (part // LANES) + b
            columns.append(state[:, at : at + 1] + square[b * LANES : (b + 1) * LANES])
        new = jnp.concatenate(columns, axis=0)
        old = table_ref[k * part : (k + 1) * part, :].astype(F32)
        out_ref[k, 0:part, :] = (old - 0.3 * total / jnp.sqrt(new)).astype(BF)
        wide = [jnp.transpose(jnp.broadcast_to(c, (LANES, LANES)))[0:IDS] for c in columns]
        wide = jnp.concatenate(wide, axis=1)
        hi, mid, lo = split3(wide)
        kind = iota((IDS, 2 * LANES), 0)
        parts = jnp.where(kind == 0, hi, jnp.where(kind == 1, mid, jnp.where(kind == 2, lo, 0.0)))
        out_ref[k, part : part + IDS, :] = parts.astype(BF)


def average_kernel(got_ref, out_ref):
    replicas, rows, embed = got_ref.shape
    part = rows - IDS
    total = got_ref[0].astype(F32)
    for r in range(1, replicas):
        total = total + got_ref[r].astype(F32)
    total = total * (1.0 / replicas)
    table = total[:part].astype(BF)
    state = total[part : part + 1] + total[part + 1 : part + 2] + total[part + 2 : part + 3]
    hi, mid, lo = split3(jnp.broadcast_to(state, (IDS, embed)))
    kind = iota((IDS, embed), 0)
    parts = jnp.where(kind == 0, hi, jnp.where(kind == 1, mid, jnp.where(kind == 2, lo, 0.0)))
    parts = parts.astype(BF)
    for r in range(replicas):
        out_ref[r, 0:part, :] = table
        out_ref[r, part:rows, :] = parts


def unpack_kernel(got_ref, table_ref, state_ref):
    shards, rows, embed = got_ref.shape
    part = rows - IDS
    for k in range(shards):
        table_ref[k * part : (k + 1) * part, :] = got_ref[k, 0:part, :]
        parts = got_ref[k, part:rows, :].astype(F32)
        state = parts[0:1] + parts[1:2] + parts[2:3]
        state_ref[k : k + 1, :] = state


PARAMS = pltpu.CompilerParams(vmem_limit_bytes=40 * 2**20)
VMEM = pl.BlockSpec(memory_space=pltpu.VMEM)
SMEM = pl.BlockSpec(memory_space=pltpu.SMEM)


def shards_fn(pooled_grad, owner_ids, local_ids, feature_table, table_rows, adagrad_state):
    samples, features, embed = pooled_grad.shape
    pool = local_ids.shape[2]
    tables, rows_dev = adagrad_state.shape
    owners = lax.axis_size("mp")
    replicas = lax.axis_size("rep")
    slots = tables * rows_dev
    count = samples * features * pool
    cap = 3 * count // (2 * owners)
    part = slots // replicas
    owner = jnp.transpose(owner_ids[..., 0], (1, 2, 0)).reshape(features * pool, samples)
    local = jnp.transpose(local_ids, (1, 2, 0)).reshape(features * pool, samples)
    send = pl.pallas_call(
        lambda *refs: pack_kernel(owners, cap, rows_dev, None, *refs),
        out_shape=jax.ShapeDtypeStruct((owners, 2 * cap + IDS, LANES), BF),
        in_specs=[SMEM, VMEM, VMEM, VMEM],
        out_specs=VMEM,
        compiler_params=PARAMS,
        name="pack",
    )(feature_table, owner, local, pooled_grad.reshape(samples * features, embed))
    received = lax.all_to_all(send, "mp", split_axis=0, concat_axis=0, tiled=True)
    updated = pl.pallas_call(
        lambda *refs: update_kernel(cap, replicas, *refs),
        out_shape=jax.ShapeDtypeStruct((replicas, part + IDS, embed), BF),
        in_specs=[VMEM, VMEM, VMEM],
        out_specs=VMEM,
        compiler_params=PARAMS,
        name="update",
    )(received, table_rows.reshape(slots, embed), adagrad_state.reshape(slots // LANES, LANES))
    mine = lax.all_to_all(updated, "rep", split_axis=0, concat_axis=0, tiled=True)
    copies = pl.pallas_call(
        average_kernel,
        out_shape=jax.ShapeDtypeStruct((replicas, part + IDS, embed), BF),
        in_specs=[VMEM],
        out_specs=VMEM,
        compiler_params=PARAMS,
        name="average",
    )(mine)
    full = lax.all_to_all(copies, "rep", split_axis=0, concat_axis=0, tiled=True)
    table, state = pl.pallas_call(
        unpack_kernel,
        out_shape=(
            jax.ShapeDtypeStruct((slots, embed), BF),
            jax.ShapeDtypeStruct((replicas, part), F32),
        ),
        in_specs=[VMEM],
        out_specs=(VMEM, VMEM),
        compiler_params=PARAMS,
        name="unpack",
    )(full)
    return table.reshape(tables, rows_dev, embed), state.reshape(tables, rows_dev)


def solution(mesh):
    placed = (
        P(("rep", "mp"), None, None),
        P(("rep", "mp"), None, None, None),
        P(("rep", "mp"), None, None),
        P(),
        P(None, "mp", None),
        P(None, "mp"),
    )
    return jax.shard_map(
        shards_fn,
        mesh=mesh,
        in_specs=placed,
        out_specs=(P(None, "mp", None), P(None, "mp")),
        check_vma=False,
    )
```

```python
import jax
import jax.numpy as jnp
from jax import lax
from jax.experimental import pallas as pl
from jax.experimental.pallas import tpu as pltpu
from jax.sharding import PartitionSpec as P

BF = jnp.bfloat16
F32 = jnp.float32
LANES = 128
IDS = 8


def iota(shape, dim):
    return lax.broadcasted_iota(jnp.int32, shape, dim)


def hot16(index, *rows):
    found = index == rows[0]
    for row in rows[1:]:
        found = found | (index == row)
    return jnp.where(found, jnp.ones((), BF), jnp.zeros((), BF))


def pack_kernel(owners, cap, rows_dev, tables_hbm, owner_hbm, local_hbm, grad_hbm, out_ref,
                tables_ref, owner_ref, local_ref, grad_ref, sems):
    pairs = (
        (owner_hbm, owner_ref),
        (tables_hbm, tables_ref),
        (local_hbm, local_ref),
        (grad_hbm, grad_ref),
    )
    copies = [pltpu.make_async_copy(a, b, sems.at[i]) for i, (a, b) in enumerate(pairs)]
    for copy in copies:
        copy.start()
    lists, samples = owner_ref.shape
    features = tables_ref.shape[0]
    pool = lists // features
    count = grad_ref.shape[0]
    copies[0].wait()
    owner = owner_ref[...]

    low = iota((samples, 2 * samples), 0)
    col = iota((samples, 2 * samples), 1)
    tri = jnp.where((low <= col), 1.0, 0.0).astype(BF)
    hot = [iota((owners, samples), 0) == owner[r : r + 1, :] for r in range(lists)]
    stacked = jnp.concatenate([jnp.where(h, 1.0, 0.0) for h in hot], axis=0).astype(BF)
    counts = jnp.dot(stacked, tri, preferred_element_type=F32)
    carry = jnp.zeros((owners, samples), F32)
    places = []
    for r in range(lists):
        block = counts[r * owners : (r + 1) * owners]
        running = block[:, :samples] + carry
        places.append(jnp.sum(jnp.where(hot[r], running, 0.0), axis=0, keepdims=True) - 1.0)
        carry = carry + block[:, samples:]
    place = jnp.concatenate(places, axis=0)

    spread = (iota((samples, count), 1) // features == iota((samples, count), 0))
    spread = jnp.where(spread, 1.0, 0.0).astype(BF)
    both = jnp.concatenate([owner.astype(F32), place], axis=0).astype(BF)
    wide = jnp.dot(both, spread, preferred_element_type=F32)
    slots = []
    lane_f = iota((lists, count), 1) % features
    slot = wide[:lists] * cap + wide[lists:]
    for p in range(pool):
        keep = iota((lists, count), 0) == lane_f * pool + p
        one = jnp.sum(jnp.where(keep, slot, 0.0), axis=0, keepdims=True)
        slots.append(jnp.broadcast_to(one, (16, count)).astype(jnp.int32).astype(jnp.int16)[0:1])

    group = 8
    rows = group * cap
    index = iota((rows, count), 0).astype(jnp.int16)
    copies[3].wait()
    grad = grad_ref[...]
    for g in range(owners // group):
        chosen = hot16(index, *[s - jnp.int16(g * rows) for s in slots])
        picked = jnp.dot(chosen, grad, preferred_element_type=F32)
        picked = picked.astype(BF)
        for k in range(group):
            part = picked[k * cap : (k + 1) * cap]
            out_ref[g * group + k, 0:cap, :] = part[:, :LANES]
            out_ref[g * group + k, cap : 2 * cap, :] = part[:, LANES:]

    copies[1].wait()
    copies[2].wait()
    table = jnp.zeros((lists, samples), jnp.int32)
    for f in range(features):
        table = jnp.where(iota((lists, samples), 0) // pool == f, tables_ref[f], table)
    target = table * rows_dev + local_ref[...]
    shift = (lax.axis_index("mp") % 8) * cap
    lane = place.astype(jnp.int32) + shift
    chunk = lane // LANES
    low_id = (target % 64).astype(F32)
    high_id = (target // 64).astype(F32)
    left, right = [], []
    kind = iota((IDS, samples), 0)
    for r in range(lists):
        row = slice(r, r + 1)
        value = jnp.where(kind < 3, low_id[row], high_id[row])
        value = jnp.where((kind % 3 == chunk[row]) & (kind < 6), value, 0.0)
        blocks = [jnp.where(owner[row] == o, value, 0.0) for o in range(owners)]
        left.append(jnp.concatenate(blocks, axis=0).astype(BF))
        right.append(jnp.where(lane[row] % LANES == iota((LANES, samples), 0), 1.0, 0.0).astype(BF))
    ids = lax.dot_general(
        jnp.concatenate(left, axis=1),
        jnp.concatenate(right, axis=1),
        (((1,), (1,)), ((), ())),
        preferred_element_type=F32,
    )
    out_ref[:, 2 * cap : 2 * cap + IDS, :] = ids.reshape(owners, IDS, LANES).astype(BF)


def update_kernel(cap, shards, recv_ref, table_ref, state_ref, out_ref):
    senders = recv_ref.shape[0]
    rows = table_ref.shape[0]
    part = rows // shards
    ids = recv_ref[:, 2 * cap : 2 * cap + IDS, :].astype(F32)
    ids = jnp.sum(ids.reshape(senders // 8, 8, IDS, LANES), axis=1)
    group = 16
    where, data = [], []
    for g in range(senders // group):
        lanes = []
        for h in range(group // 8):
            x = ids[g * (group // 8) + h]
            lanes += [x[j : j + 1] + 64.0 * x[j + 3 : j + 4] for j in range(3)]
        one = jnp.concatenate(lanes, axis=1)
        one = jnp.broadcast_to(one, (16, group * cap)).astype(jnp.int32).astype(jnp.int16)
        where.append(one[0:1])
        block = recv_ref[g * group : (g + 1) * group, 0 : 2 * cap, :]
        halves = [
            block[:, h * cap : (h + 1) * cap, :].reshape(group * cap, LANES) for h in range(2)
        ]
        data.append(jnp.concatenate(halves, axis=1))
    state = jnp.transpose(state_ref[...])
    index = iota((part, group * cap), 0).astype(jnp.int16)
    spread = []
    for k in range(shards):
        total = jnp.zeros((part, 2 * LANES), F32)
        for g in range(senders // group):
            hot = hot16(index, where[g] - jnp.int16(k * part))
            total = total + jnp.dot(hot, data[g], preferred_element_type=F32)
        square = jnp.sum(total * total, axis=1, keepdims=True) * (1.0 / (2 * LANES))
        columns = []
        for b in range(part // LANES):
            at = k * (part // LANES) + b
            columns.append(state[:, at : at + 1] + square[b * LANES : (b + 1) * LANES])
        new = jnp.concatenate(columns, axis=0)
        old = table_ref[k * part : (k + 1) * part, :].astype(F32)
        out_ref[k, 0:part, :] = (old - 0.3 * total / jnp.sqrt(new)).astype(BF)
        wide = [jnp.transpose(jnp.broadcast_to(c, (LANES, LANES)))[0:1] for c in columns]
        spread.append(jnp.concatenate(wide, axis=1))
    whole = jnp.concatenate(spread, axis=0)
    high = whole.astype(BF).astype(F32)
    both = jnp.concatenate([high, whole - high], axis=0).astype(BF)
    for k in range(shards):
        out_ref[k, part : part + 2 * shards, :] = both


def average_kernel(got_ref, out_ref, state_ref):
    replicas, rows, embed = got_ref.shape
    part = rows - 2 * replicas
    total = got_ref[0].astype(F32)
    for r in range(1, replicas):
        total = total + got_ref[r].astype(F32)
    total = total * (1.0 / replicas)
    table = total[:part].astype(BF)
    for r in range(replicas):
        out_ref[r, :, :] = table
    state = total[part : part + replicas] + total[part + replicas :]
    wide = state_ref.shape[1] // embed
    for k in range(replicas):
        at = (k % wide) * embed
        state_ref[k // wide : k // wide + 1, at : at + embed] = state[k : k + 1]


ALL_VMEM = pltpu.CompilerParams(vmem_limit_bytes=60 * 2**20)
PARAMS = pltpu.CompilerParams(vmem_limit_bytes=32 * 2**20)
VMEM = pl.BlockSpec(memory_space=pltpu.VMEM)
ANY = pl.BlockSpec(memory_space=pl.ANY)


def shards_fn(pooled_grad, owner_ids, local_ids, feature_table, table_rows, adagrad_state):
    samples, features, embed = pooled_grad.shape
    pool = local_ids.shape[2]
    tables, rows_dev = adagrad_state.shape
    owners = lax.axis_size("mp")
    replicas = lax.axis_size("rep")
    slots = tables * rows_dev
    count = samples * features * pool
    cap = 3 * count // (2 * owners)
    part = slots // replicas
    owner = jnp.transpose(owner_ids[..., 0], (1, 2, 0)).reshape(features * pool, samples)
    local = jnp.transpose(local_ids, (1, 2, 0)).reshape(features * pool, samples)
    send = pl.pallas_call(
        lambda *refs: pack_kernel(owners, cap, rows_dev, *refs),
        out_shape=jax.ShapeDtypeStruct((owners, 2 * cap + IDS, LANES), BF),
        in_specs=[ANY, ANY, ANY, ANY],
        out_specs=VMEM,
        scratch_shapes=[
            pltpu.SMEM((features,), jnp.int32),
            pltpu.VMEM((features * pool, samples), jnp.int32),
            pltpu.VMEM((features * pool, samples), jnp.int32),
            pltpu.VMEM((samples * features, embed), BF),
            pltpu.SemaphoreType.DMA((4,)),
        ],
        compiler_params=ALL_VMEM,
        name="pack",
    )(feature_table, owner, local, pooled_grad.reshape(samples * features, embed))
    received = lax.all_to_all(send, "mp", split_axis=0, concat_axis=0, tiled=True)
    updated = pl.pallas_call(
        lambda *refs: update_kernel(cap, replicas, *refs),
        out_shape=jax.ShapeDtypeStruct((replicas, part + 2 * replicas, embed), BF),
        in_specs=[VMEM, VMEM, VMEM],
        out_specs=VMEM,
        compiler_params=PARAMS,
        name="update",
    )(received, table_rows.reshape(slots, embed), adagrad_state.reshape(slots // LANES, LANES))
    mine = lax.all_to_all(updated, "rep", split_axis=0, concat_axis=0, tiled=True)
    copies, state = pl.pallas_call(
        average_kernel,
        out_shape=(
            jax.ShapeDtypeStruct((replicas, part, embed), BF),
            jax.ShapeDtypeStruct((tables, rows_dev), F32),
        ),
        in_specs=[VMEM],
        out_specs=(VMEM, VMEM),
        compiler_params=PARAMS,
        name="average",
    )(mine)
    full = lax.all_to_all(copies, "rep", split_axis=0, concat_axis=0, tiled=True)
    return full.reshape(tables, rows_dev, embed), state


def solution(mesh):
    placed = (
        P(("rep", "mp"), None, None),
        P(("rep", "mp"), None, None, None),
        P(("rep", "mp"), None, None),
        P(),
        P(None, "mp", None),
        P(None, "mp"),
    )
    return jax.shard_map(
        shards_fn,
        mesh=mesh,
        in_specs=placed,
        out_specs=(P(None, "mp", None), P(None, "mp")),
        check_vma=False,
    )
```

```python
import jax
import jax.numpy as jnp
from jax import lax
from jax.experimental import pallas as pl
from jax.experimental.pallas import tpu as pltpu
from jax.sharding import PartitionSpec as P

BF = jnp.bfloat16
F32 = jnp.float32
LANES = 128
TURNS = 2
IDS = 8


def iota(shape, dim):
    return lax.broadcasted_iota(jnp.int32, shape, dim)


def hot16(index, *rows):
    found = index == rows[0]
    for row in rows[1:]:
        found = found | (index == row)
    return jnp.where(found, jnp.ones((), BF), jnp.zeros((), BF))


def pack_kernel(owners, cap, rows_dev, tables_hbm, owner_hbm, local_hbm, grad_hbm, own_ref,
                other_ref, tables_ref, owner_ref, local_ref, grad_ref, sems):
    chips = owners // 2
    pairs = (
        (owner_hbm, owner_ref),
        (tables_hbm, tables_ref),
        (local_hbm, local_ref),
        (grad_hbm, grad_ref),
    )
    copies = [pltpu.make_async_copy(a, b, sems.at[i]) for i, (a, b) in enumerate(pairs)]
    for copy in copies:
        copy.start()
    lists, samples = owner_ref.shape
    features = tables_ref.shape[0]
    pool = lists // features
    count = grad_ref.shape[0]
    copies[0].wait()
    owner = owner_ref[...]
    core = lax.axis_index("core")
    owner = owner // 2 + chips * ((owner + core) % 2)

    low = iota((samples, 2 * samples), 0)
    col = iota((samples, 2 * samples), 1)
    tri = jnp.where((low <= col), 1.0, 0.0).astype(BF)
    hot = [iota((owners, samples), 0) == owner[r : r + 1, :] for r in range(lists)]
    stacked = jnp.concatenate([jnp.where(h, 1.0, 0.0) for h in hot], axis=0).astype(BF)
    counts = jnp.dot(stacked, tri, preferred_element_type=F32)
    carry = jnp.zeros((owners, samples), F32)
    places = []
    for r in range(lists):
        block = counts[r * owners : (r + 1) * owners]
        running = block[:, :samples] + carry
        places.append(jnp.sum(jnp.where(hot[r], running, 0.0), axis=0, keepdims=True) - 1.0)
        carry = carry + block[:, samples:]
    place = jnp.concatenate(places, axis=0)

    spread = (iota((samples, count), 1) // features == iota((samples, count), 0))
    spread = jnp.where(spread, 1.0, 0.0).astype(BF)
    both = jnp.concatenate([owner.astype(F32), place], axis=0).astype(BF)
    wide = jnp.dot(both, spread, preferred_element_type=F32)
    slots = []
    lane_f = iota((lists, count), 1) % features
    slot = wide[:lists] * cap + wide[lists:]
    for p in range(pool):
        keep = iota((lists, count), 0) == lane_f * pool + p
        one = jnp.sum(jnp.where(keep, slot, 0.0), axis=0, keepdims=True)
        slots.append(jnp.broadcast_to(one, (16, count)).astype(jnp.int32).astype(jnp.int16)[0:1])

    group = 8
    rows = group * cap
    index = iota((rows, count), 0).astype(jnp.int16)
    copies[3].wait()
    grad = grad_ref[...]
    for g in range(owners // group):
        chosen = hot16(index, *[s - jnp.int16(g * rows) for s in slots])
        picked = jnp.dot(chosen, grad, preferred_element_type=F32)
        picked = picked.astype(BF)
        for k in range(group):
            part = picked[k * cap : (k + 1) * cap]
            out_ref, at = (own_ref, other_ref)[(g * group + k) // chips], (g * group + k) % chips
            out_ref[at, 0:cap, :] = part[:, :LANES]
            out_ref[at, cap : 2 * cap, :] = part[:, LANES:]

    copies[1].wait()
    copies[2].wait()
    table = jnp.zeros((lists, samples), jnp.int32)
    for f in range(features):
        table = jnp.where(iota((lists, samples), 0) // pool == f, tables_ref[f], table)
    target = table * rows_dev + local_ref[...]
    shift = ((lax.axis_index("yx") % 4) * 2 + core) * cap
    lane = place.astype(jnp.int32) + shift
    chunk = lane // LANES
    low_id = (target % 64).astype(F32)
    high_id = (target // 64).astype(F32)
    left, right = [], []
    kind = iota((IDS, samples), 0)
    for r in range(lists):
        row = slice(r, r + 1)
        value = jnp.where(kind < 3, low_id[row], high_id[row])
        value = jnp.where((kind % 3 == chunk[row]) & (kind < 6), value, 0.0)
        blocks = [jnp.where(owner[row] == o, value, 0.0) for o in range(owners)]
        left.append(jnp.concatenate(blocks, axis=0).astype(BF))
        right.append(jnp.where(lane[row] % LANES == iota((LANES, samples), 0), 1.0, 0.0).astype(BF))
    ids = lax.dot_general(
        jnp.concatenate(left, axis=1),
        jnp.concatenate(right, axis=1),
        (((1,), (1,)), ((), ())),
        preferred_element_type=F32,
    )
    ids = ids.reshape(owners, IDS, LANES).astype(BF)
    own_ref[:, 2 * cap : 2 * cap + IDS, :] = ids[:chips]
    other_ref[:, 2 * cap : 2 * cap + IDS, :] = ids[chips:]


def merge_kernel(own_ref, got_ref, turn_ref, out_ref):
    rows = own_ref.shape[1] - IDS
    first = lax.axis_index("core") == 0

    @pl.when(first)
    def _():
        out_ref[:, 0:rows, :] = own_ref[:, 0:rows, :]
        out_ref[:, rows : 2 * rows, :] = got_ref[:, 0:rows, :]

    @pl.when(jnp.logical_not(first))
    def _():
        out_ref[:, 0:rows, :] = got_ref[:, 0:rows, :]
        out_ref[:, rows : 2 * rows, :] = own_ref[:, 0:rows, :]

    ids = own_ref[:, rows:, :].astype(F32) + got_ref[:, rows:, :].astype(F32)
    out_ref[:, 2 * rows :, :] = ids.astype(BF)
    turn = jnp.where(iota((IDS, LANES), 0) < 6, ids[0], turn_ref[...].astype(F32))
    out_ref[0, 2 * rows :, :] = turn.astype(BF)


def update_kernel(cap, shards, recv_ref, table_ref, state_ref, out_ref):
    chips = recv_ref.shape[0]
    senders = 2 * chips
    rows = table_ref.shape[0]
    part = rows // shards
    ids = recv_ref[:, 4 * cap : 4 * cap + IDS, :].astype(F32)
    ids = jnp.sum(ids.reshape(chips // 4, 4, IDS, LANES), axis=1)
    group = 16
    where, data = [], []
    for g in range(senders // group):
        lanes = []
        for h in range(group // 8):
            x = ids[g * (group // 8) + h]
            lanes += [x[j : j + 1] + 64.0 * x[j + 3 : j + 4] for j in range(3)]
        one = jnp.concatenate(lanes, axis=1)
        one = jnp.broadcast_to(one, (16, group * cap)).astype(jnp.int32).astype(jnp.int16)
        where.append(one[0:1])
        block = recv_ref[g * group // 2 : (g + 1) * group // 2, 0 : 4 * cap, :]
        block = block.reshape(group, 2 * cap, LANES)
        halves = [
            block[:, h * cap : (h + 1) * cap, :].reshape(group * cap, LANES) for h in range(2)
        ]
        data.append(jnp.concatenate(halves, axis=1))
    state = jnp.transpose(state_ref[...])
    index = iota((part, group * cap), 0).astype(jnp.int16)
    spread = []
    for k in range(shards):
        total = jnp.zeros((part, 2 * LANES), F32)
        for g in range(senders // group):
            hot = hot16(index, where[g] - jnp.int16(k * part))
            total = total + jnp.dot(hot, data[g], preferred_element_type=F32)
        square = jnp.sum(total * total, axis=1, keepdims=True) * (1.0 / (2 * LANES))
        columns = []
        for b in range(part // LANES):
            at = k * (part // LANES) + b
            columns.append(state[:, at : at + 1] + square[b * LANES : (b + 1) * LANES])
        new = jnp.concatenate(columns, axis=0)
        old = table_ref[k * part : (k + 1) * part, :].astype(F32)
        out_ref[k, 0:part, :] = (old - 0.3 * total / jnp.sqrt(new)).astype(BF)
        wide = [jnp.transpose(jnp.broadcast_to(c, (LANES, LANES)))[0:1] for c in columns]
        spread.append(jnp.concatenate(wide, axis=1))
    whole = jnp.concatenate(spread, axis=0)
    high = whole.astype(BF).astype(F32)
    both = jnp.concatenate([high, whole - high], axis=0).astype(BF)
    for k in range(shards):
        out_ref[k, part : part + 2 * shards, :] = both


def average_kernel(got_ref, out_ref, state_ref):
    replicas, rows, embed = got_ref.shape
    part = rows - 2 * replicas
    total = got_ref[0].astype(F32)
    for r in range(1, replicas):
        total = total + got_ref[r].astype(F32)
    total = total * (1.0 / replicas)
    table = total[:part].astype(BF)
    for r in range(replicas):
        out_ref[r, :, :] = table
    state = total[part : part + replicas] + total[part + replicas :]
    wide = state_ref.shape[1] // embed
    for k in range(replicas):
        at = (k % wide) * embed
        state_ref[k // wide : k // wide + 1, at : at + embed] = state[k : k + 1]


ALL_VMEM = pltpu.CompilerParams(vmem_limit_bytes=60 * 2**20)
PARAMS = pltpu.CompilerParams(vmem_limit_bytes=32 * 2**20)
VMEM = pl.BlockSpec(memory_space=pltpu.VMEM)
ANY = pl.BlockSpec(memory_space=pl.ANY)


def shards_fn(pooled_grad, owner_ids, local_ids, feature_table, table_rows, adagrad_state):
    samples, features, embed = pooled_grad.shape
    pool = local_ids.shape[2]
    tables, rows_dev = adagrad_state.shape
    chips = lax.axis_size("yx")
    owners = 2 * chips
    replicas = lax.axis_size("rep")
    slots = tables * rows_dev
    count = samples * features * pool
    cap = 3 * count // (2 * owners)
    part = slots // replicas
    owner = jnp.transpose(owner_ids[..., 0], (1, 2, 0)).reshape(features * pool, samples)
    local = jnp.transpose(local_ids, (1, 2, 0)).reshape(features * pool, samples)
    own, other = pl.pallas_call(
        lambda *refs: pack_kernel(owners, cap, rows_dev, *refs),
        out_shape=(jax.ShapeDtypeStruct((chips, 2 * cap + IDS, LANES), BF),) * 2,
        in_specs=[ANY, ANY, ANY, ANY],
        out_specs=(VMEM, VMEM),
        scratch_shapes=[
            pltpu.SMEM((features,), jnp.int32),
            pltpu.VMEM((features * pool, samples), jnp.int32),
            pltpu.VMEM((features * pool, samples), jnp.int32),
            pltpu.VMEM((samples * features, embed), BF),
            pltpu.SemaphoreType.DMA((4,)),
        ],
        compiler_params=ALL_VMEM,
        name="pack",
    )(feature_table, owner, local, pooled_grad.reshape(samples * features, embed))
    got = lax.ppermute(other, "core", [(0, 1), (1, 0)])
    turn = got[0, 2 * cap :, :]
    for _ in range(TURNS):
        ring = [(2 * i + 1, 2 * ((i + 1) % chips) + 1) for i in range(chips)]
        turn = lax.ppermute(turn, ("yx", "core"), ring)
    send = pl.pallas_call(
        merge_kernel,
        out_shape=jax.ShapeDtypeStruct((chips, 4 * cap + IDS, LANES), BF),
        in_specs=[VMEM, VMEM, VMEM],
        out_specs=VMEM,
        compiler_params=PARAMS,
        name="merge",
    )(own, got, turn)
    received = lax.all_to_all(send, "yx", split_axis=0, concat_axis=0, tiled=True)
    updated = pl.pallas_call(
        lambda *refs: update_kernel(cap, replicas, *refs),
        out_shape=jax.ShapeDtypeStruct((replicas, part + 2 * replicas, embed), BF),
        in_specs=[VMEM, VMEM, VMEM],
        out_specs=VMEM,
        compiler_params=PARAMS,
        name="update",
    )(received, table_rows.reshape(slots, embed), adagrad_state.reshape(slots // LANES, LANES))
    mine = lax.all_to_all(updated, "rep", split_axis=0, concat_axis=0, tiled=True)
    copies, state = pl.pallas_call(
        average_kernel,
        out_shape=(
            jax.ShapeDtypeStruct((replicas, part, embed), BF),
            jax.ShapeDtypeStruct((tables, rows_dev), F32),
        ),
        in_specs=[VMEM],
        out_specs=(VMEM, VMEM),
        compiler_params=PARAMS,
        name="average",
    )(mine)
    full = lax.all_to_all(copies, "rep", split_axis=0, concat_axis=0, tiled=True)
    return full.reshape(tables, rows_dev, embed), state


def solution(mesh):
    replicas, owners = mesh.devices.shape
    cores = mesh.devices.reshape(replicas, owners // 2, 2)
    by_core = jax.sharding.Mesh(cores, ("rep", "yx", "core"))
    every, mine = ("rep", "yx", "core"), ("yx", "core")
    placed = (
        P(every, None, None),
        P(every, None, None, None),
        P(every, None, None),
        P(),
        P(None, mine, None),
        P(None, mine),
    )
    return jax.shard_map(
        shards_fn,
        mesh=by_core,
        in_specs=placed,
        out_specs=(P(None, mine, None), P(None, mine)),
        check_vma=False,
    )
```

```python
import jax
import jax.numpy as jnp
from jax import lax
from jax.experimental import pallas as pl
from jax.experimental.pallas import tpu as pltpu
from jax.sharding import PartitionSpec as P

BF = jnp.bfloat16
F32 = jnp.float32
LANES = 128
TURNS = 1
IDS = 8


def iota(shape, dim):
    return lax.broadcasted_iota(jnp.int32, shape, dim)


def hot16(index, *rows):
    found = index == rows[0]
    for row in rows[1:]:
        found = found | (index == row)
    return jnp.where(found, jnp.ones((), BF), jnp.zeros((), BF))


def pack_kernel(owners, cap, rows_dev, tables_hbm, owner_hbm, local_hbm, grad_hbm, own_ref,
                other_ref, tables_ref, owner_ref, local_ref, grad_ref, sems):
    chips = owners // 2
    pairs = (
        (owner_hbm, owner_ref),
        (tables_hbm, tables_ref),
        (local_hbm, local_ref),
        (grad_hbm, grad_ref),
    )
    copies = [pltpu.make_async_copy(a, b, sems.at[i]) for i, (a, b) in enumerate(pairs)]
    for copy in copies:
        copy.start()
    lists, samples = owner_ref.shape
    features = tables_ref.shape[0]
    pool = lists // features
    count = grad_ref.shape[0]
    copies[0].wait()
    owner = owner_ref[...]
    core = lax.axis_index("core")
    owner = owner // 2 + chips * ((owner + core) % 2)

    low = iota((samples, 2 * samples), 0)
    col = iota((samples, 2 * samples), 1)
    tri = jnp.where((low <= col), 1.0, 0.0).astype(BF)
    hot = [iota((owners, samples), 0) == owner[r : r + 1, :] for r in range(lists)]
    stacked = jnp.concatenate([jnp.where(h, 1.0, 0.0) for h in hot], axis=0).astype(BF)
    counts = jnp.dot(stacked, tri, preferred_element_type=F32)
    carry = jnp.zeros((owners, samples), F32)
    places = []
    for r in range(lists):
        block = counts[r * owners : (r + 1) * owners]
        running = block[:, :samples] + carry
        places.append(jnp.sum(jnp.where(hot[r], running, 0.0), axis=0, keepdims=True) - 1.0)
        carry = carry + block[:, samples:]
    place = jnp.concatenate(places, axis=0)

    spread = (iota((samples, count), 1) // features == iota((samples, count), 0))
    spread = jnp.where(spread, 1.0, 0.0).astype(BF)
    both = jnp.concatenate([owner.astype(F32), place], axis=0).astype(BF)
    wide = jnp.dot(both, spread, preferred_element_type=F32)
    slots = []
    lane_f = iota((lists, count), 1) % features
    slot = wide[:lists] * cap + wide[lists:]
    for p in range(pool):
        keep = iota((lists, count), 0) == lane_f * pool + p
        one = jnp.sum(jnp.where(keep, slot, 0.0), axis=0, keepdims=True)
        slots.append(jnp.broadcast_to(one, (16, count)).astype(jnp.int32).astype(jnp.int16)[0:1])

    group = 8
    rows = group * cap
    index = iota((rows, count), 0).astype(jnp.int16)
    copies[3].wait()
    grad = grad_ref[...]
    for g in range(owners // group):
        chosen = hot16(index, *[s - jnp.int16(g * rows) for s in slots])
        picked = jnp.dot(chosen, grad, preferred_element_type=F32)
        picked = picked.astype(BF)
        for k in range(group):
            part = picked[k * cap : (k + 1) * cap]
            out_ref, at = (own_ref, other_ref)[(g * group + k) // chips], (g * group + k) % chips
            out_ref[at, 0:cap, :] = part[:, :LANES]
            out_ref[at, cap : 2 * cap, :] = part[:, LANES:]

    copies[1].wait()
    copies[2].wait()
    table = jnp.zeros((lists, samples), jnp.int32)
    for f in range(features):
        table = jnp.where(iota((lists, samples), 0) // pool == f, tables_ref[f], table)
    target = table * rows_dev + local_ref[...]
    shift = ((lax.axis_index("yx") % 4) * 2 + core) * cap
    lane = place.astype(jnp.int32) + shift
    chunk = lane // LANES
    low_id = (target % 64).astype(F32)
    high_id = (target // 64).astype(F32)
    left, right = [], []
    kind = iota((IDS, samples), 0)
    for r in range(lists):
        row = slice(r, r + 1)
        value = jnp.where(kind < 3, low_id[row], high_id[row])
        value = jnp.where((kind % 3 == chunk[row]) & (kind < 6), value, 0.0)
        blocks = [jnp.where(owner[row] == o, value, 0.0) for o in range(owners)]
        left.append(jnp.concatenate(blocks, axis=0).astype(BF))
        right.append(jnp.where(lane[row] % LANES == iota((LANES, samples), 0), 1.0, 0.0).astype(BF))
    ids = lax.dot_general(
        jnp.concatenate(left, axis=1),
        jnp.concatenate(right, axis=1),
        (((1,), (1,)), ((), ())),
        preferred_element_type=F32,
    )
    ids = ids.reshape(owners, IDS, LANES).astype(BF)
    own_ref[:, 2 * cap : 2 * cap + IDS, :] = ids[:chips]
    other_ref[:, 2 * cap : 2 * cap + IDS, :] = ids[chips:]


def merge_kernel(own_ref, got_ref, turn_ref, out_ref):
    rows = own_ref.shape[1] - IDS
    first = lax.axis_index("core") == 0

    @pl.when(first)
    def _():
        out_ref[:, 0:rows, :] = own_ref[:, 0:rows, :]
        out_ref[:, rows : 2 * rows, :] = got_ref[:, 0:rows, :]

    @pl.when(jnp.logical_not(first))
    def _():
        out_ref[:, 0:rows, :] = got_ref[:, 0:rows, :]
        out_ref[:, rows : 2 * rows, :] = own_ref[:, 0:rows, :]

    ids = own_ref[:, rows:, :].astype(F32) + got_ref[:, rows:, :].astype(F32)
    out_ref[:, 2 * rows :, :] = ids.astype(BF)
    turn = jnp.where(iota((IDS, LANES), 0) < 6, ids[0], turn_ref[...].astype(F32))
    out_ref[0, 2 * rows :, :] = turn.astype(BF)


def update_kernel(cap, shards, recv_ref, table_ref, state_ref, out_ref):
    chips = recv_ref.shape[0]
    senders = 2 * chips
    rows = table_ref.shape[0]
    part = rows // shards
    ids = recv_ref[:, 4 * cap : 4 * cap + IDS, :].astype(F32)
    ids = jnp.sum(ids.reshape(chips // 4, 4, IDS, LANES), axis=1)
    group = 16
    where, data = [], []
    for g in range(senders // group):
        lanes = []
        for h in range(group // 8):
            x = ids[g * (group // 8) + h]
            lanes += [x[j : j + 1] + 64.0 * x[j + 3 : j + 4] for j in range(3)]
        one = jnp.concatenate(lanes, axis=1)
        one = jnp.broadcast_to(one, (16, group * cap)).astype(jnp.int32).astype(jnp.int16)
        where.append(one[0:1])
        block = recv_ref[g * group // 2 : (g + 1) * group // 2, 0 : 4 * cap, :]
        block = block.reshape(group, 2 * cap, LANES)
        halves = [
            block[:, h * cap : (h + 1) * cap, :].reshape(group * cap, LANES) for h in range(2)
        ]
        data.append(jnp.concatenate(halves, axis=1))
    state = jnp.transpose(state_ref[...])
    index = iota((part, group * cap), 0).astype(jnp.int16)
    spread = []
    for k in range(shards):
        total = jnp.zeros((part, 2 * LANES), F32)
        for g in range(senders // group):
            hot = hot16(index, where[g] - jnp.int16(k * part))
            total = total + jnp.dot(hot, data[g], preferred_element_type=F32)
        square = jnp.sum(total * total, axis=1, keepdims=True) * (1.0 / (2 * LANES))
        columns = []
        for b in range(part // LANES):
            at = k * (part // LANES) + b
            columns.append(state[:, at : at + 1] + square[b * LANES : (b + 1) * LANES])
        new = jnp.concatenate(columns, axis=0)
        old = table_ref[k * part : (k + 1) * part, :].astype(F32)
        out_ref[k, 0:part, :] = (old - 0.3 * total / jnp.sqrt(new)).astype(BF)
        wide = [jnp.transpose(jnp.broadcast_to(c, (LANES, LANES)))[0:1] for c in columns]
        spread.append(jnp.concatenate(wide, axis=1))
    whole = jnp.concatenate(spread, axis=0)
    high = whole.astype(BF).astype(F32)
    both = jnp.concatenate([high, whole - high], axis=0).astype(BF)
    for k in range(shards):
        out_ref[k, part : part + 2 * shards, :] = both


def average_kernel(got_ref, out_ref, state_ref):
    replicas, rows, embed = got_ref.shape
    part = rows - 2 * replicas
    total = got_ref[0].astype(F32)
    for r in range(1, replicas):
        total = total + got_ref[r].astype(F32)
    total = total * (1.0 / replicas)
    table = total[:part].astype(BF)
    for r in range(replicas):
        out_ref[r, :, :] = table
    state = total[part : part + replicas] + total[part + replicas :]
    wide = state_ref.shape[1] // embed
    for k in range(replicas):
        at = (k % wide) * embed
        state_ref[k // wide : k // wide + 1, at : at + embed] = state[k : k + 1]


ALL_VMEM = pltpu.CompilerParams(vmem_limit_bytes=60 * 2**20)
PARAMS = pltpu.CompilerParams(vmem_limit_bytes=32 * 2**20)
VMEM = pl.BlockSpec(memory_space=pltpu.VMEM)
ANY = pl.BlockSpec(memory_space=pl.ANY)


def shards_fn(pooled_grad, owner_ids, local_ids, feature_table, table_rows, adagrad_state):
    samples, features, embed = pooled_grad.shape
    pool = local_ids.shape[2]
    tables, rows_dev = adagrad_state.shape
    chips = lax.axis_size("yx")
    owners = 2 * chips
    replicas = lax.axis_size("rep")
    slots = tables * rows_dev
    count = samples * features * pool
    cap = 3 * count // (2 * owners)
    part = slots // replicas
    owner = jnp.transpose(owner_ids[..., 0], (1, 2, 0)).reshape(features * pool, samples)
    local = jnp.transpose(local_ids, (1, 2, 0)).reshape(features * pool, samples)
    own, other = pl.pallas_call(
        lambda *refs: pack_kernel(owners, cap, rows_dev, *refs),
        out_shape=(jax.ShapeDtypeStruct((chips, 2 * cap + IDS, LANES), BF),) * 2,
        in_specs=[ANY, ANY, ANY, ANY],
        out_specs=(VMEM, VMEM),
        scratch_shapes=[
            pltpu.SMEM((features,), jnp.int32),
            pltpu.VMEM((features * pool, samples), jnp.int32),
            pltpu.VMEM((features * pool, samples), jnp.int32),
            pltpu.VMEM((samples * features, embed), BF),
            pltpu.SemaphoreType.DMA((4,)),
        ],
        compiler_params=ALL_VMEM,
        name="pack",
    )(feature_table, owner, local, pooled_grad.reshape(samples * features, embed))
    got = lax.ppermute(other, "core", [(0, 1), (1, 0)])
    turn = got[0, 2 * cap :, :]
    for _ in range(TURNS):
        ring = [(2 * i + 1, 2 * ((i + 1) % chips) + 1) for i in range(chips)]
        turn = lax.ppermute(turn, ("yx", "core"), ring)
    send = pl.pallas_call(
        merge_kernel,
        out_shape=jax.ShapeDtypeStruct((chips, 4 * cap + IDS, LANES), BF),
        in_specs=[VMEM, VMEM, VMEM],
        out_specs=VMEM,
        compiler_params=PARAMS,
        name="merge",
    )(own, got, turn)
    received = lax.all_to_all(send, "yx", split_axis=0, concat_axis=0, tiled=True)
    updated = pl.pallas_call(
        lambda *refs: update_kernel(cap, replicas, *refs),
        out_shape=jax.ShapeDtypeStruct((replicas, part + 2 * replicas, embed), BF),
        in_specs=[VMEM, VMEM, VMEM],
        out_specs=VMEM,
        compiler_params=PARAMS,
        name="update",
    )(received, table_rows.reshape(slots, embed), adagrad_state.reshape(slots // LANES, LANES))
    mine = lax.all_to_all(updated, "rep", split_axis=0, concat_axis=0, tiled=True)
    copies, state = pl.pallas_call(
        average_kernel,
        out_shape=(
            jax.ShapeDtypeStruct((replicas, part, embed), BF),
            jax.ShapeDtypeStruct((tables, rows_dev), F32),
        ),
        in_specs=[VMEM],
        out_specs=(VMEM, VMEM),
        compiler_params=PARAMS,
        name="average",
    )(mine)
    full = lax.all_to_all(copies, "rep", split_axis=0, concat_axis=0, tiled=True)
    return full.reshape(tables, rows_dev, embed), state


def solution(mesh):
    replicas, owners = mesh.devices.shape
    cores = mesh.devices.reshape(replicas, owners // 2, 2)
    by_core = jax.sharding.Mesh(cores, ("rep", "yx", "core"))
    every, mine = ("rep", "yx", "core"), ("yx", "core")
    placed = (
        P(every, None, None),
        P(every, None, None, None),
        P(every, None, None),
        P(),
        P(None, mine, None),
        P(None, mine),
    )
    return jax.shard_map(
        shards_fn,
        mesh=by_core,
        in_specs=placed,
        out_specs=(P(None, mine, None), P(None, mine)),
        check_vma=False,
    )
```

```python
import jax
import jax.numpy as jnp
from jax import lax
from jax.experimental import pallas as pl
from jax.experimental.pallas import tpu as pltpu
from jax.sharding import PartitionSpec as P

BF = jnp.bfloat16
F32 = jnp.float32
LANES = 128
TURNS = 2
IDS = 8


def iota(shape, dim):
    return lax.broadcasted_iota(jnp.int32, shape, dim)


def hot16(index, *rows):
    found = index == rows[0]
    for row in rows[1:]:
        found = found | (index == row)
    return jnp.where(found, jnp.ones((), BF), jnp.zeros((), BF))


def pack_kernel(owners, cap, rows_dev, tables_hbm, owner_hbm, local_hbm, grad_hbm, own_ref,
                other_ref, turn_ref, tables_ref, owner_ref, local_ref, grad_ref, sems):
    chips = owners // 2
    pairs = (
        (owner_hbm, owner_ref),
        (tables_hbm, tables_ref),
        (local_hbm, local_ref),
        (grad_hbm, grad_ref),
    )
    copies = [pltpu.make_async_copy(a, b, sems.at[i]) for i, (a, b) in enumerate(pairs)]
    for copy in copies:
        copy.start()
    lists, samples = owner_ref.shape
    features = tables_ref.shape[0]
    pool = lists // features
    count = grad_ref.shape[0]
    copies[0].wait()
    owner = owner_ref[...]
    core = lax.axis_index("core")
    owner = owner // 2 + chips * ((owner + core) % 2)

    low = iota((samples, 2 * samples), 0)
    col = iota((samples, 2 * samples), 1)
    tri = jnp.where((low <= col), 1.0, 0.0).astype(BF)
    hot = [iota((owners, samples), 0) == owner[r : r + 1, :] for r in range(lists)]
    stacked = jnp.concatenate([jnp.where(h, 1.0, 0.0) for h in hot], axis=0).astype(BF)
    counts = jnp.dot(stacked, tri, preferred_element_type=F32)
    carry = jnp.zeros((owners, samples), F32)
    places = []
    for r in range(lists):
        block = counts[r * owners : (r + 1) * owners]
        running = block[:, :samples] + carry
        places.append(jnp.sum(jnp.where(hot[r], running, 0.0), axis=0, keepdims=True) - 1.0)
        carry = carry + block[:, samples:]
    place = jnp.concatenate(places, axis=0)

    spread = (iota((samples, count), 1) // features == iota((samples, count), 0))
    spread = jnp.where(spread, 1.0, 0.0).astype(BF)
    both = jnp.concatenate([owner.astype(F32), place], axis=0).astype(BF)
    wide = jnp.dot(both, spread, preferred_element_type=F32)
    slots = []
    lane_f = iota((lists, count), 1) % features
    slot = wide[:lists] * cap + wide[lists:]
    for p in range(pool):
        keep = iota((lists, count), 0) == lane_f * pool + p
        one = jnp.sum(jnp.where(keep, slot, 0.0), axis=0, keepdims=True)
        slots.append(jnp.broadcast_to(one, (16, count)).astype(jnp.int32).astype(jnp.int16)[0:1])

    group = 8
    rows = group * cap
    index = iota((rows, count), 0).astype(jnp.int16)
    copies[3].wait()
    grad = grad_ref[...]
    for g in range(owners // group):
        chosen = hot16(index, *[s - jnp.int16(g * rows) for s in slots])
        picked = jnp.dot(chosen, grad, preferred_element_type=F32)
        picked = picked.astype(BF)
        for k in range(group):
            part = picked[k * cap : (k + 1) * cap]
            out_ref, at = (own_ref, other_ref)[(g * group + k) // chips], (g * group + k) % chips
            out_ref[at, 0:cap, :] = part[:, :LANES]
            out_ref[at, cap : 2 * cap, :] = part[:, LANES:]

    copies[1].wait()
    copies[2].wait()
    table = jnp.zeros((lists, samples), jnp.int32)
    for f in range(features):
        table = jnp.where(iota((lists, samples), 0) // pool == f, tables_ref[f], table)
    target = table * rows_dev + local_ref[...]
    shift = ((lax.axis_index("yx") % 4) * 2 + core) * cap
    lane = place.astype(jnp.int32) + shift
    chunk = lane // LANES
    low_id = (target % 64).astype(F32)
    high_id = (target // 64).astype(F32)
    left, right = [], []
    kind = iota((IDS, samples), 0)
    for r in range(lists):
        row = slice(r, r + 1)
        value = jnp.where(kind < 3, low_id[row], high_id[row])
        value = jnp.where((kind % 3 == chunk[row]) & (kind < 6), value, 0.0)
        blocks = [jnp.where(owner[row] == o, value, 0.0) for o in range(owners)]
        left.append(jnp.concatenate(blocks, axis=0).astype(BF))
        right.append(jnp.where(lane[row] % LANES == iota((LANES, samples), 0), 1.0, 0.0).astype(BF))
    ids = lax.dot_general(
        jnp.concatenate(left, axis=1),
        jnp.concatenate(right, axis=1),
        (((1,), (1,)), ((), ())),
        preferred_element_type=F32,
    )
    ids = ids.reshape(owners, IDS, LANES).astype(BF)
    own_ref[:, 2 * cap : 2 * cap + IDS, :] = ids[:chips]
    other_ref[:, 2 * cap : 2 * cap + IDS, :] = ids[chips:]
    turn_ref[...] = jnp.zeros((IDS, LANES), BF)


def merge_kernel(own_ref, got_ref, turn_ref, out_ref):
    rows = own_ref.shape[1] - IDS
    first = lax.axis_index("core") == 0

    @pl.when(first)
    def _():
        out_ref[:, 0:rows, :] = own_ref[:, 0:rows, :]
        out_ref[:, rows : 2 * rows, :] = got_ref[:, 0:rows, :]

    @pl.when(jnp.logical_not(first))
    def _():
        out_ref[:, 0:rows, :] = got_ref[:, 0:rows, :]
        out_ref[:, rows : 2 * rows, :] = own_ref[:, 0:rows, :]

    ids = own_ref[:, rows:, :].astype(F32) + got_ref[:, rows:, :].astype(F32)
    out_ref[:, 2 * rows :, :] = ids.astype(BF)
    turn = jnp.where(iota((IDS, LANES), 0) < 6, ids[0], turn_ref[...].astype(F32))
    out_ref[0, 2 * rows :, :] = turn.astype(BF)


def update_kernel(cap, shards, recv_ref, table_ref, state_ref, out_ref):
    chips = recv_ref.shape[0]
    senders = 2 * chips
    rows = table_ref.shape[0]
    part = rows // shards
    ids = recv_ref[:, 4 * cap : 4 * cap + IDS, :].astype(F32)
    ids = jnp.sum(ids.reshape(chips // 4, 4, IDS, LANES), axis=1)
    group = 16
    where, data = [], []
    for g in range(senders // group):
        lanes = []
        for h in range(group // 8):
            x = ids[g * (group // 8) + h]
            lanes += [x[j : j + 1] + 64.0 * x[j + 3 : j + 4] for j in range(3)]
        one = jnp.concatenate(lanes, axis=1)
        one = jnp.broadcast_to(one, (16, group * cap)).astype(jnp.int32).astype(jnp.int16)
        where.append(one[0:1])
        block = recv_ref[g * group // 2 : (g + 1) * group // 2, 0 : 4 * cap, :]
        block = block.reshape(group, 2 * cap, LANES)
        halves = [
            block[:, h * cap : (h + 1) * cap, :].reshape(group * cap, LANES) for h in range(2)
        ]
        data.append(jnp.concatenate(halves, axis=1))
    state = jnp.transpose(state_ref[...])
    index = iota((part, group * cap), 0).astype(jnp.int16)
    spread = []
    for k in range(shards):
        total = jnp.zeros((part, 2 * LANES), F32)
        for g in range(senders // group):
            hot = hot16(index, where[g] - jnp.int16(k * part))
            total = total + jnp.dot(hot, data[g], preferred_element_type=F32)
        square = jnp.sum(total * total, axis=1, keepdims=True) * (1.0 / (2 * LANES))
        columns = []
        for b in range(part // LANES):
            at = k * (part // LANES) + b
            columns.append(state[:, at : at + 1] + square[b * LANES : (b + 1) * LANES])
        new = jnp.concatenate(columns, axis=0)
        old = table_ref[k * part : (k + 1) * part, :].astype(F32)
        out_ref[k, 0:part, :] = (old - 0.3 * total / jnp.sqrt(new)).astype(BF)
        wide = [jnp.transpose(jnp.broadcast_to(c, (LANES, LANES)))[0:1] for c in columns]
        spread.append(jnp.concatenate(wide, axis=1))
    whole = jnp.concatenate(spread, axis=0)
    high = whole.astype(BF).astype(F32)
    both = jnp.concatenate([high, whole - high], axis=0).astype(BF)
    for k in range(shards):
        out_ref[k, part : part + 2 * shards, :] = both


def average_kernel(got_ref, out_ref, state_ref):
    replicas, rows, embed = got_ref.shape
    part = rows - 2 * replicas
    total = got_ref[0].astype(F32)
    for r in range(1, replicas):
        total = total + got_ref[r].astype(F32)
    total = total * (1.0 / replicas)
    table = total[:part].astype(BF)
    for r in range(replicas):
        out_ref[r, :, :] = table
    state = total[part : part + replicas] + total[part + replicas :]
    wide = state_ref.shape[1] // embed
    for k in range(replicas):
        at = (k % wide) * embed
        state_ref[k // wide : k // wide + 1, at : at + embed] = state[k : k + 1]


ALL_VMEM = pltpu.CompilerParams(vmem_limit_bytes=60 * 2**20)
PARAMS = pltpu.CompilerParams(vmem_limit_bytes=32 * 2**20)
VMEM = pl.BlockSpec(memory_space=pltpu.VMEM)
ANY = pl.BlockSpec(memory_space=pl.ANY)


def shards_fn(pooled_grad, owner_ids, local_ids, feature_table, table_rows, adagrad_state):
    samples, features, embed = pooled_grad.shape
    pool = local_ids.shape[2]
    tables, rows_dev = adagrad_state.shape
    chips = lax.axis_size("yx")
    owners = 2 * chips
    replicas = lax.axis_size("rep")
    slots = tables * rows_dev
    count = samples * features * pool
    cap = 3 * count // (2 * owners)
    part = slots // replicas
    owner = jnp.transpose(owner_ids[..., 0], (1, 2, 0)).reshape(features * pool, samples)
    local = jnp.transpose(local_ids, (1, 2, 0)).reshape(features * pool, samples)
    own, other, turn = pl.pallas_call(
        lambda *refs: pack_kernel(owners, cap, rows_dev, *refs),
        out_shape=(
            jax.ShapeDtypeStruct((chips, 2 * cap + IDS, LANES), BF),
            jax.ShapeDtypeStruct((chips, 2 * cap + IDS, LANES), BF),
            jax.ShapeDtypeStruct((IDS, LANES), BF),
        ),
        in_specs=[ANY, ANY, ANY, ANY],
        out_specs=(VMEM, VMEM, VMEM),
        scratch_shapes=[
            pltpu.SMEM((features,), jnp.int32),
            pltpu.VMEM((features * pool, samples), jnp.int32),
            pltpu.VMEM((features * pool, samples), jnp.int32),
            pltpu.VMEM((samples * features, embed), BF),
            pltpu.SemaphoreType.DMA((4,)),
        ],
        compiler_params=ALL_VMEM,
        name="pack",
    )(feature_table, owner, local, pooled_grad.reshape(samples * features, embed))
    got = lax.ppermute(other, "core", [(0, 1), (1, 0)])
    for _ in range(TURNS):
        ring = [(2 * i + 1, 2 * ((i + 1) % chips) + 1) for i in range(chips)]
        turn = lax.ppermute(turn, ("yx", "core"), ring)
    send = pl.pallas_call(
        merge_kernel,
        out_shape=jax.ShapeDtypeStruct((chips, 4 * cap + IDS, LANES), BF),
        in_specs=[VMEM, VMEM, VMEM],
        out_specs=VMEM,
        compiler_params=PARAMS,
        name="merge",
    )(own, got, turn)
    received = lax.all_to_all(send, "yx", split_axis=0, concat_axis=0, tiled=True)
    updated = pl.pallas_call(
        lambda *refs: update_kernel(cap, replicas, *refs),
        out_shape=jax.ShapeDtypeStruct((replicas, part + 2 * replicas, embed), BF),
        in_specs=[VMEM, VMEM, VMEM],
        out_specs=VMEM,
        compiler_params=PARAMS,
        name="update",
    )(received, table_rows.reshape(slots, embed), adagrad_state.reshape(slots // LANES, LANES))
    mine = lax.all_to_all(updated, "rep", split_axis=0, concat_axis=0, tiled=True)
    copies, state = pl.pallas_call(
        average_kernel,
        out_shape=(
            jax.ShapeDtypeStruct((replicas, part, embed), BF),
            jax.ShapeDtypeStruct((tables, rows_dev), F32),
        ),
        in_specs=[VMEM],
        out_specs=(VMEM, VMEM),
        compiler_params=PARAMS,
        name="average",
    )(mine)
    full = lax.all_to_all(copies, "rep", split_axis=0, concat_axis=0, tiled=True)
    return full.reshape(tables, rows_dev, embed), state


def solution(mesh):
    replicas, owners = mesh.devices.shape
    cores = mesh.devices.reshape(replicas, owners // 2, 2)
    by_core = jax.sharding.Mesh(cores, ("rep", "yx", "core"))
    every, mine = ("rep", "yx", "core"), ("yx", "core")
    placed = (
        P(every, None, None),
        P(every, None, None, None),
        P(every, None, None),
        P(),
        P(None, mine, None),
        P(None, mine),
    )
    return jax.shard_map(
        shards_fn,
        mesh=by_core,
        in_specs=placed,
        out_specs=(P(None, mine, None), P(None, mine)),
        check_vma=False,
    )
```

```python
import jax
import jax.numpy as jnp
from jax import lax
from jax.experimental import pallas as pl
from jax.experimental.pallas import tpu as pltpu
from jax.sharding import PartitionSpec as P

BF = jnp.bfloat16
F32 = jnp.float32
LANES = 128
TURNS = 2
IDS = 8


def iota(shape, dim):
    return lax.broadcasted_iota(jnp.int32, shape, dim)


def hot16(index, *rows):
    found = index == rows[0]
    for row in rows[1:]:
        found = found | (index == row)
    return jnp.where(found, jnp.ones((), BF), jnp.zeros((), BF))


def pack_kernel(owners, cap, rows_dev, tables_hbm, owner_hbm, local_hbm, grad_hbm, own_hbm,
                other_hbm, turn_ref, own_ref, other_ref, tables_ref, owner_ref, local_ref,
                grad_ref, sems, out_sems):
    chips = owners // 2
    pairs = (
        (owner_hbm, owner_ref),
        (tables_hbm, tables_ref),
        (local_hbm, local_ref),
        (grad_hbm, grad_ref),
    )
    copies = [pltpu.make_async_copy(a, b, sems.at[i]) for i, (a, b) in enumerate(pairs)]
    for copy in copies:
        copy.start()
    lists, samples = owner_ref.shape
    features = tables_ref.shape[0]
    pool = lists // features
    count = grad_ref.shape[0]
    copies[0].wait()
    owner = owner_ref[...]
    core = lax.axis_index("core")
    owner = owner // 2 + chips * ((owner + core) % 2)

    low = iota((samples, 2 * samples), 0)
    col = iota((samples, 2 * samples), 1)
    tri = jnp.where((low <= col), 1.0, 0.0).astype(BF)
    hot = [iota((owners, samples), 0) == owner[r : r + 1, :] for r in range(lists)]
    stacked = jnp.concatenate([jnp.where(h, 1.0, 0.0) for h in hot], axis=0).astype(BF)
    counts = jnp.dot(stacked, tri, preferred_element_type=F32)
    carry = jnp.zeros((owners, samples), F32)
    places = []
    for r in range(lists):
        block = counts[r * owners : (r + 1) * owners]
        running = block[:, :samples] + carry
        places.append(jnp.sum(jnp.where(hot[r], running, 0.0), axis=0, keepdims=True) - 1.0)
        carry = carry + block[:, samples:]
    place = jnp.concatenate(places, axis=0)

    spread = (iota((samples, count), 1) // features == iota((samples, count), 0))
    spread = jnp.where(spread, 1.0, 0.0).astype(BF)
    both = jnp.concatenate([owner.astype(F32), place], axis=0).astype(BF)
    wide = jnp.dot(both, spread, preferred_element_type=F32)
    slots = []
    lane_f = iota((lists, count), 1) % features
    slot = wide[:lists] * cap + wide[lists:]
    for p in range(pool):
        keep = iota((lists, count), 0) == lane_f * pool + p
        one = jnp.sum(jnp.where(keep, slot, 0.0), axis=0, keepdims=True)
        slots.append(jnp.broadcast_to(one, (16, count)).astype(jnp.int32).astype(jnp.int16)[0:1])

    copies[1].wait()
    copies[2].wait()
    table = jnp.zeros((lists, samples), jnp.int32)
    for f in range(features):
        table = jnp.where(iota((lists, samples), 0) // pool == f, tables_ref[f], table)
    target = table * rows_dev + local_ref[...]
    shift = ((lax.axis_index("yx") % 4) * 2 + core) * cap
    lane = place.astype(jnp.int32) + shift
    chunk = lane // LANES
    low_id = (target % 64).astype(F32)
    high_id = (target // 64).astype(F32)
    left, right = [], []
    kind = iota((IDS, samples), 0)
    for r in range(lists):
        row = slice(r, r + 1)
        value = jnp.where(kind < 3, low_id[row], high_id[row])
        value = jnp.where((kind % 3 == chunk[row]) & (kind < 6), value, 0.0)
        blocks = [jnp.where(owner[row] == o, value, 0.0) for o in range(owners)]
        left.append(jnp.concatenate(blocks, axis=0).astype(BF))
        right.append(jnp.where(lane[row] % LANES == iota((LANES, samples), 0), 1.0, 0.0).astype(BF))
    ids = lax.dot_general(
        jnp.concatenate(left, axis=1),
        jnp.concatenate(right, axis=1),
        (((1,), (1,)), ((), ())),
        preferred_element_type=F32,
    )
    ids = ids.reshape(owners, IDS, LANES).astype(BF)
    own_ref[:, 2 * cap : 2 * cap + IDS, :] = ids[:chips]
    other_ref[:, 2 * cap : 2 * cap + IDS, :] = ids[chips:]
    turn_ref[...] = jnp.zeros((IDS, LANES), BF)

    group = 8
    rows = group * cap
    index = iota((rows, count), 0).astype(jnp.int16)
    copies[3].wait()
    grad = grad_ref[...]
    writes = []
    for g in range(owners // group - 1, -1, -1):
        chosen = hot16(index, *[s - jnp.int16(g * rows) for s in slots])
        picked = jnp.dot(chosen, grad, preferred_element_type=F32)
        picked = picked.astype(BF)
        for k in range(group):
            part = picked[k * cap : (k + 1) * cap]
            out_ref, at = (own_ref, other_ref)[(g * group + k) // chips], (g * group + k) % chips
            out_ref[at, 0:cap, :] = part[:, :LANES]
            out_ref[at, cap : 2 * cap, :] = part[:, LANES:]
        side = g * group // chips
        some = pl.ds(g * group % chips, group)
        write = pltpu.make_async_copy(
            (own_ref, other_ref)[side].at[some], (own_hbm, other_hbm)[side].at[some], out_sems.at[g]
        )
        write.start()
        writes.append(write)
    for write in writes:
        write.wait()


def place_kernel(own_ref, out_ref):
    out_ref[...] = own_ref[...]


def merge_kernel(own_ref, got_ref, turn_ref, out_ref):
    rows = own_ref.shape[1] - IDS
    first = lax.axis_index("core") == 0

    @pl.when(first)
    def _():
        out_ref[:, 0:rows, :] = own_ref[:, 0:rows, :]
        out_ref[:, rows : 2 * rows, :] = got_ref[:, 0:rows, :]

    @pl.when(jnp.logical_not(first))
    def _():
        out_ref[:, 0:rows, :] = got_ref[:, 0:rows, :]
        out_ref[:, rows : 2 * rows, :] = own_ref[:, 0:rows, :]

    ids = own_ref[:, rows:, :].astype(F32) + got_ref[:, rows:, :].astype(F32)
    out_ref[:, 2 * rows :, :] = ids.astype(BF)
    turn = jnp.where(iota((IDS, LANES), 0) < 6, ids[0], turn_ref[...].astype(F32))
    out_ref[0, 2 * rows :, :] = turn.astype(BF)


def update_kernel(cap, shards, recv_ref, table_ref, state_ref, out_ref):
    chips = recv_ref.shape[0]
    senders = 2 * chips
    rows = table_ref.shape[0]
    part = rows // shards
    ids = recv_ref[:, 4 * cap : 4 * cap + IDS, :].astype(F32)
    ids = jnp.sum(ids.reshape(chips // 4, 4, IDS, LANES), axis=1)
    group = 16
    where, data = [], []
    for g in range(senders // group):
        lanes = []
        for h in range(group // 8):
            x = ids[g * (group // 8) + h]
            lanes += [x[j : j + 1] + 64.0 * x[j + 3 : j + 4] for j in range(3)]
        one = jnp.concatenate(lanes, axis=1)
        one = jnp.broadcast_to(one, (16, group * cap)).astype(jnp.int32).astype(jnp.int16)
        where.append(one[0:1])
        block = recv_ref[g * group // 2 : (g + 1) * group // 2, 0 : 4 * cap, :]
        block = block.reshape(group, 2 * cap, LANES)
        halves = [
            block[:, h * cap : (h + 1) * cap, :].reshape(group * cap, LANES) for h in range(2)
        ]
        data.append(jnp.concatenate(halves, axis=1))
    state = jnp.transpose(state_ref[...])
    index = iota((part, group * cap), 0).astype(jnp.int16)
    spread = []
    for k in range(shards):
        total = jnp.zeros((part, 2 * LANES), F32)
        for g in range(senders // group):
            hot = hot16(index, where[g] - jnp.int16(k * part))
            total = total + jnp.dot(hot, data[g], preferred_element_type=F32)
        square = jnp.sum(total * total, axis=1, keepdims=True) * (1.0 / (2 * LANES))
        columns = []
        for b in range(part // LANES):
            at = k * (part // LANES) + b
            columns.append(state[:, at : at + 1] + square[b * LANES : (b + 1) * LANES])
        new = jnp.concatenate(columns, axis=0)
        old = table_ref[k * part : (k + 1) * part, :].astype(F32)
        out_ref[k, 0:part, :] = (old - 0.3 * total / jnp.sqrt(new)).astype(BF)
        wide = [jnp.transpose(jnp.broadcast_to(c, (LANES, LANES)))[0:1] for c in columns]
        spread.append(jnp.concatenate(wide, axis=1))
    whole = jnp.concatenate(spread, axis=0)
    high = whole.astype(BF).astype(F32)
    both = jnp.concatenate([high, whole - high], axis=0).astype(BF)
    for k in range(shards):
        out_ref[k, part : part + 2 * shards, :] = both


def average_kernel(got_ref, out_ref):
    replicas, part, _ = out_ref.shape
    total = got_ref[0, 0:part, :].astype(F32)
    for r in range(1, replicas):
        total = total + got_ref[r, 0:part, :].astype(F32)
    table = (total * (1.0 / replicas)).astype(BF)
    for r in range(replicas):
        out_ref[r, :, :] = table


def state_kernel(got_ref, state_ref):
    replicas, rows, embed = got_ref.shape
    part = rows - 2 * replicas
    total = got_ref[0, part:, :].astype(F32)
    for r in range(1, replicas):
        total = total + got_ref[r, part:, :].astype(F32)
    state = (total[:replicas] + total[replicas:]) * (1.0 / replicas)
    wide = state_ref.shape[1] // embed
    for k in range(replicas):
        at = (k % wide) * embed
        state_ref[k // wide : k // wide + 1, at : at + embed] = state[k : k + 1]


ALL_VMEM = pltpu.CompilerParams(vmem_limit_bytes=60 * 2**20)
PARAMS = pltpu.CompilerParams(vmem_limit_bytes=32 * 2**20)
VMEM = pl.BlockSpec(memory_space=pltpu.VMEM)
ANY = pl.BlockSpec(memory_space=pl.ANY)


def shards_fn(pooled_grad, owner_ids, local_ids, feature_table, table_rows, adagrad_state):
    samples, features, embed = pooled_grad.shape
    pool = local_ids.shape[2]
    tables, rows_dev = adagrad_state.shape
    chips = lax.axis_size("yx")
    owners = 2 * chips
    replicas = lax.axis_size("rep")
    slots = tables * rows_dev
    count = samples * features * pool
    cap = 3 * count // (2 * owners)
    part = slots // replicas
    owner = jnp.transpose(owner_ids[..., 0], (1, 2, 0)).reshape(features * pool, samples)
    local = jnp.transpose(local_ids, (1, 2, 0)).reshape(features * pool, samples)
    own, other, turn = pl.pallas_call(
        lambda *refs: pack_kernel(owners, cap, rows_dev, *refs),
        out_shape=(
            jax.ShapeDtypeStruct((chips, 2 * cap + IDS, LANES), BF),
            jax.ShapeDtypeStruct((chips, 2 * cap + IDS, LANES), BF),
            jax.ShapeDtypeStruct((IDS, LANES), BF),
        ),
        in_specs=[ANY, ANY, ANY, ANY],
        out_specs=(ANY, ANY, VMEM),
        scratch_shapes=[
            pltpu.VMEM((chips, 2 * cap + IDS, LANES), BF),
            pltpu.VMEM((chips, 2 * cap + IDS, LANES), BF),
            pltpu.SMEM((features,), jnp.int32),
            pltpu.VMEM((features * pool, samples), jnp.int32),
            pltpu.VMEM((features * pool, samples), jnp.int32),
            pltpu.VMEM((samples * features, embed), BF),
            pltpu.SemaphoreType.DMA((4,)),
            pltpu.SemaphoreType.DMA((owners // 8,)),
        ],
        compiler_params=ALL_VMEM,
        name="pack",
    )(feature_table, owner, local, pooled_grad.reshape(samples * features, embed))
    got = lax.ppermute(other, "core", [(0, 1), (1, 0)])
    for _ in range(TURNS):
        ring = [(2 * i + 1, 2 * ((i + 1) % chips) + 1) for i in range(chips)]
        turn = lax.ppermute(turn, ("yx", "core"), ring)
    placed = pl.pallas_call(
        place_kernel,
        out_shape=jax.ShapeDtypeStruct((chips, 2 * cap + IDS, LANES), BF),
        in_specs=[VMEM],
        out_specs=VMEM,
        compiler_params=PARAMS,
        name="place",
    )(own)
    send = pl.pallas_call(
        merge_kernel,
        out_shape=jax.ShapeDtypeStruct((chips, 4 * cap + IDS, LANES), BF),
        in_specs=[VMEM, VMEM, VMEM],
        out_specs=VMEM,
        compiler_params=PARAMS,
        name="merge",
    )(placed, got, turn)
    received = lax.all_to_all(send, "yx", split_axis=0, concat_axis=0, tiled=True)
    updated = pl.pallas_call(
        lambda *refs: update_kernel(cap, replicas, *refs),
        out_shape=jax.ShapeDtypeStruct((replicas, part + 2 * replicas, embed), BF),
        in_specs=[VMEM, VMEM, VMEM],
        out_specs=VMEM,
        compiler_params=PARAMS,
        name="update",
    )(received, table_rows.reshape(slots, embed), adagrad_state.reshape(slots // LANES, LANES))
    mine = lax.all_to_all(updated, "rep", split_axis=0, concat_axis=0, tiled=True)
    copies = pl.pallas_call(
        average_kernel,
        out_shape=jax.ShapeDtypeStruct((replicas, part, embed), BF),
        in_specs=[VMEM],
        out_specs=VMEM,
        compiler_params=PARAMS,
        name="average",
    )(mine)
    state = pl.pallas_call(
        state_kernel,
        out_shape=jax.ShapeDtypeStruct((tables, rows_dev), F32),
        in_specs=[VMEM],
        out_specs=VMEM,
        compiler_params=PARAMS,
        name="state",
    )(mine)
    full = lax.all_to_all(copies, "rep", split_axis=0, concat_axis=0, tiled=True)
    return full.reshape(tables, rows_dev, embed), state


def solution(mesh):
    replicas, owners = mesh.devices.shape
    cores = mesh.devices.reshape(replicas, owners // 2, 2)
    by_core = jax.sharding.Mesh(cores, ("rep", "yx", "core"))
    every, mine = ("rep", "yx", "core"), ("yx", "core")
    placed = (
        P(every, None, None),
        P(every, None, None, None),
        P(every, None, None),
        P(),
        P(None, mine, None),
        P(None, mine),
    )
    return jax.shard_map(
        shards_fn,
        mesh=by_core,
        in_specs=placed,
        out_specs=(P(None, mine, None), P(None, mine)),
        check_vma=False,
    )
```

```python
import jax
import jax.numpy as jnp
from jax import lax
from jax.experimental import pallas as pl
from jax.experimental.pallas import tpu as pltpu
from jax.sharding import PartitionSpec as P

BF = jnp.bfloat16
F32 = jnp.float32
LANES = 128
TURNS = 2
IDS = 8


def iota(shape, dim):
    return lax.broadcasted_iota(jnp.int32, shape, dim)


def hot16(index, *rows):
    found = index == rows[0]
    for row in rows[1:]:
        found = found | (index == row)
    return jnp.where(found, jnp.ones((), BF), jnp.zeros((), BF))


def pack_kernel(owners, cap, rows_dev, tables_hbm, owner_hbm, local_hbm, grad_hbm, own_ref,
                other_ref, turn_ref, tables_ref, owner_ref, local_ref, grad_ref, sems):
    chips = owners // 2
    pairs = (
        (owner_hbm, owner_ref),
        (tables_hbm, tables_ref),
        (local_hbm, local_ref),
        (grad_hbm, grad_ref),
    )
    copies = [pltpu.make_async_copy(a, b, sems.at[i]) for i, (a, b) in enumerate(pairs)]
    for copy in copies:
        copy.start()
    lists, samples = owner_ref.shape
    features = tables_ref.shape[0]
    pool = lists // features
    count = grad_ref.shape[0]
    copies[0].wait()
    owner = owner_ref[...]
    core = lax.axis_index("core")
    owner = owner // 2 + chips * ((owner + core) % 2)

    low = iota((samples, 2 * samples), 0)
    col = iota((samples, 2 * samples), 1)
    tri = jnp.where((low <= col), 1.0, 0.0).astype(BF)
    hot = [iota((owners, samples), 0) == owner[r : r + 1, :] for r in range(lists)]
    stacked = jnp.concatenate([jnp.where(h, 1.0, 0.0) for h in hot], axis=0).astype(BF)
    counts = jnp.dot(stacked, tri, preferred_element_type=F32)
    carry = jnp.zeros((owners, samples), F32)
    places = []
    for r in range(lists):
        block = counts[r * owners : (r + 1) * owners]
        running = block[:, :samples] + carry
        places.append(jnp.sum(jnp.where(hot[r], running, 0.0), axis=0, keepdims=True) - 1.0)
        carry = carry + block[:, samples:]
    place = jnp.concatenate(places, axis=0)

    spread = (iota((samples, count), 1) // features == iota((samples, count), 0))
    spread = jnp.where(spread, 1.0, 0.0).astype(BF)
    both = jnp.concatenate([owner.astype(F32), place], axis=0).astype(BF)
    wide = jnp.dot(both, spread, preferred_element_type=F32)
    slots = []
    lane_f = iota((lists, count), 1) % features
    slot = wide[:lists] * cap + wide[lists:]
    for p in range(pool):
        keep = iota((lists, count), 0) == lane_f * pool + p
        one = jnp.sum(jnp.where(keep, slot, 0.0), axis=0, keepdims=True)
        slots.append(jnp.broadcast_to(one, (16, count)).astype(jnp.int32).astype(jnp.int16)[0:1])

    group = 8
    rows = group * cap
    index = iota((rows, count), 0).astype(jnp.int16)
    copies[3].wait()
    grad = grad_ref[...]
    for g in range(owners // group):
        chosen = hot16(index, *[s - jnp.int16(g * rows) for s in slots])
        picked = jnp.dot(chosen, grad, preferred_element_type=F32)
        picked = picked.astype(BF)
        for k in range(group):
            part = picked[k * cap : (k + 1) * cap]
            out_ref, at = (own_ref, other_ref)[(g * group + k) // chips], (g * group + k) % chips
            out_ref[at, 0:cap, :] = part[:, :LANES]
            out_ref[at, cap : 2 * cap, :] = part[:, LANES:]

    copies[1].wait()
    copies[2].wait()
    table = jnp.zeros((lists, samples), jnp.int32)
    for f in range(features):
        table = jnp.where(iota((lists, samples), 0) // pool == f, tables_ref[f], table)
    target = table * rows_dev + local_ref[...]
    shift = ((lax.axis_index("yx") % 4) * 2 + core) * cap
    lane = place.astype(jnp.int32) + shift
    chunk = lane // LANES
    low_id = (target % 64).astype(F32)
    high_id = (target // 64).astype(F32)
    left, right = [], []
    kind = iota((IDS, samples), 0)
    for r in range(lists):
        row = slice(r, r + 1)
        value = jnp.where(kind < 3, low_id[row], high_id[row])
        value = jnp.where((kind % 3 == chunk[row]) & (kind < 6), value, 0.0)
        blocks = [jnp.where(owner[row] == o, value, 0.0) for o in range(owners)]
        left.append(jnp.concatenate(blocks, axis=0).astype(BF))
        right.append(jnp.where(lane[row] % LANES == iota((LANES, samples), 0), 1.0, 0.0).astype(BF))
    ids = lax.dot_general(
        jnp.concatenate(left, axis=1),
        jnp.concatenate(right, axis=1),
        (((1,), (1,)), ((), ())),
        preferred_element_type=F32,
    )
    ids = ids.reshape(owners, IDS, LANES).astype(BF)
    own_ref[:, 2 * cap : 2 * cap + IDS, :] = ids[:chips]
    other_ref[:, 2 * cap : 2 * cap + IDS, :] = ids[chips:]
    turn_ref[...] = jnp.zeros((IDS, LANES), BF)


def place_kernel(own_ref, out_ref):
    out_ref[...] = own_ref[...]


def merge_kernel(own_ref, got_ref, turn_ref, out_ref, sem):
    rows = own_ref.shape[1] - IDS
    core = lax.axis_index("core")

    def merge(own_at, got_at):
        came = got_ref.at[:, pl.ds(0, rows), :]
        copy = pltpu.make_async_copy(came, out_ref.at[:, pl.ds(got_at, rows), :], sem)
        copy.start()
        out_ref[:, own_at : own_at + rows, :] = own_ref[:, 0:rows, :]
        ids = own_ref[:, rows:, :].astype(F32) + got_ref[:, rows:, :].astype(F32)
        out_ref[:, 2 * rows :, :] = ids.astype(BF)
        turn = jnp.where(iota((IDS, LANES), 0) < 6, ids[0], turn_ref[...].astype(F32))
        out_ref[0, 2 * rows :, :] = turn.astype(BF)
        copy.wait()

    @pl.when(core == 0)
    def _():
        merge(0, rows)

    @pl.when(core == 1)
    def _():
        merge(rows, 0)


def update_kernel(cap, shards, recv_ref, table_ref, state_ref, out_ref):
    chips = recv_ref.shape[0]
    senders = 2 * chips
    rows = table_ref.shape[0]
    part = rows // shards
    ids = recv_ref[:, 4 * cap : 4 * cap + IDS, :].astype(F32)
    ids = jnp.sum(ids.reshape(chips // 4, 4, IDS, LANES), axis=1)
    group = 16
    where, data = [], []
    for g in range(senders // group):
        lanes = []
        for h in range(group // 8):
            x = ids[g * (group // 8) + h]
            lanes += [x[j : j + 1] + 64.0 * x[j + 3 : j + 4] for j in range(3)]
        one = jnp.concatenate(lanes, axis=1)
        one = jnp.broadcast_to(one, (16, group * cap)).astype(jnp.int32).astype(jnp.int16)
        where.append(one[0:1])
        block = recv_ref[g * group // 2 : (g + 1) * group // 2, 0 : 4 * cap, :]
        block = block.reshape(group, 2 * cap, LANES)
        halves = [
            block[:, h * cap : (h + 1) * cap, :].reshape(group * cap, LANES) for h in range(2)
        ]
        data.append(jnp.concatenate(halves, axis=1))
    state = jnp.transpose(state_ref[...])
    index = iota((part, group * cap), 0).astype(jnp.int16)
    spread = []
    for k in range(shards):
        total = jnp.zeros((part, 2 * LANES), F32)
        for g in range(senders // group):
            hot = hot16(index, where[g] - jnp.int16(k * part))
            total = total + jnp.dot(hot, data[g], preferred_element_type=F32)
        square = jnp.sum(total * total, axis=1, keepdims=True) * (1.0 / (2 * LANES))
        columns = []
        for b in range(part // LANES):
            at = k * (part // LANES) + b
            columns.append(state[:, at : at + 1] + square[b * LANES : (b + 1) * LANES])
        new = jnp.concatenate(columns, axis=0)
        old = table_ref[k * part : (k + 1) * part, :].astype(F32)
        out_ref[k, 0:part, :] = (old - 0.3 * total / jnp.sqrt(new)).astype(BF)
        wide = [jnp.transpose(jnp.broadcast_to(c, (LANES, LANES)))[0:1] for c in columns]
        spread.append(jnp.concatenate(wide, axis=1))
    whole = jnp.concatenate(spread, axis=0)
    high = whole.astype(BF).astype(F32)
    both = jnp.concatenate([high, whole - high], axis=0).astype(BF)
    for k in range(shards):
        out_ref[k, part : part + 2 * shards, :] = both


def average_kernel(got_ref, out_ref, state_ref):
    replicas, rows, embed = got_ref.shape
    part = rows - 2 * replicas
    total = got_ref[0].astype(F32)
    for r in range(1, replicas):
        total = total + got_ref[r].astype(F32)
    total = total * (1.0 / replicas)
    table = total[:part].astype(BF)
    for r in range(replicas):
        out_ref[r, :, :] = table
    state = total[part : part + replicas] + total[part + replicas :]
    wide = state_ref.shape[1] // embed
    for k in range(replicas):
        at = (k % wide) * embed
        state_ref[k // wide : k // wide + 1, at : at + embed] = state[k : k + 1]


ALL_VMEM = pltpu.CompilerParams(vmem_limit_bytes=60 * 2**20)
PARAMS = pltpu.CompilerParams(vmem_limit_bytes=32 * 2**20)
VMEM = pl.BlockSpec(memory_space=pltpu.VMEM)
ANY = pl.BlockSpec(memory_space=pl.ANY)


def shards_fn(pooled_grad, owner_ids, local_ids, feature_table, table_rows, adagrad_state):
    samples, features, embed = pooled_grad.shape
    pool = local_ids.shape[2]
    tables, rows_dev = adagrad_state.shape
    chips = lax.axis_size("yx")
    owners = 2 * chips
    replicas = lax.axis_size("rep")
    slots = tables * rows_dev
    count = samples * features * pool
    cap = 3 * count // (2 * owners)
    part = slots // replicas
    owner = jnp.transpose(owner_ids[..., 0], (1, 2, 0)).reshape(features * pool, samples)
    local = jnp.transpose(local_ids, (1, 2, 0)).reshape(features * pool, samples)
    own, other, turn = pl.pallas_call(
        lambda *refs: pack_kernel(owners, cap, rows_dev, *refs),
        out_shape=(
            jax.ShapeDtypeStruct((chips, 2 * cap + IDS, LANES), BF),
            jax.ShapeDtypeStruct((chips, 2 * cap + IDS, LANES), BF),
            jax.ShapeDtypeStruct((IDS, LANES), BF),
        ),
        in_specs=[ANY, ANY, ANY, ANY],
        out_specs=(VMEM, VMEM, VMEM),
        scratch_shapes=[
            pltpu.SMEM((features,), jnp.int32),
            pltpu.VMEM((features * pool, samples), jnp.int32),
            pltpu.VMEM((features * pool, samples), jnp.int32),
            pltpu.VMEM((samples * features, embed), BF),
            pltpu.SemaphoreType.DMA((4,)),
        ],
        compiler_params=ALL_VMEM,
        name="pack",
    )(feature_table, owner, local, pooled_grad.reshape(samples * features, embed))
    got = lax.ppermute(other, "core", [(0, 1), (1, 0)])
    for _ in range(TURNS):
        ring = [(2 * i + 1, 2 * ((i + 1) % chips) + 1) for i in range(chips)]
        turn = lax.ppermute(turn, ("yx", "core"), ring)
    placed = pl.pallas_call(
        place_kernel,
        out_shape=jax.ShapeDtypeStruct(own.shape, BF),
        in_specs=[VMEM],
        out_specs=VMEM,
        compiler_params=PARAMS,
        name="place",
    )(own)
    send = pl.pallas_call(
        merge_kernel,
        out_shape=jax.ShapeDtypeStruct((chips, 4 * cap + IDS, LANES), BF),
        in_specs=[VMEM, VMEM, VMEM],
        out_specs=VMEM,
        scratch_shapes=[pltpu.SemaphoreType.DMA],
        compiler_params=PARAMS,
        name="merge",
    )(placed, got, turn)
    received = lax.all_to_all(send, "yx", split_axis=0, concat_axis=0, tiled=True)
    updated = pl.pallas_call(
        lambda *refs: update_kernel(cap, replicas, *refs),
        out_shape=jax.ShapeDtypeStruct((replicas, part + 2 * replicas, embed), BF),
        in_specs=[VMEM, VMEM, VMEM],
        out_specs=VMEM,
        compiler_params=PARAMS,
        name="update",
    )(received, table_rows.reshape(slots, embed), adagrad_state.reshape(slots // LANES, LANES))
    mine = lax.all_to_all(updated, "rep", split_axis=0, concat_axis=0, tiled=True)
    copies, state = pl.pallas_call(
        average_kernel,
        out_shape=(
            jax.ShapeDtypeStruct((replicas, part, embed), BF),
            jax.ShapeDtypeStruct((tables, rows_dev), F32),
        ),
        in_specs=[VMEM],
        out_specs=(VMEM, VMEM),
        compiler_params=PARAMS,
        name="average",
    )(mine)
    full = lax.all_to_all(copies, "rep", split_axis=0, concat_axis=0, tiled=True)
    return full.reshape(tables, rows_dev, embed), state


def solution(mesh):
    replicas, owners = mesh.devices.shape
    cores = mesh.devices.reshape(replicas, owners // 2, 2)
    by_core = jax.sharding.Mesh(cores, ("rep", "yx", "core"))
    every, mine = ("rep", "yx", "core"), ("yx", "core")
    placed = (
        P(every, None, None),
        P(every, None, None, None),
        P(every, None, None),
        P(),
        P(None, mine, None),
        P(None, mine),
    )
    return jax.shard_map(
        shards_fn,
        mesh=by_core,
        in_specs=placed,
        out_specs=(P(None, mine, None), P(None, mine)),
        check_vma=False,
    )
```

```python
import jax
import jax.numpy as jnp
from jax import lax
from jax.experimental import pallas as pl
from jax.experimental.pallas import tpu as pltpu
from jax.sharding import PartitionSpec as P

BF = jnp.bfloat16
F32 = jnp.float32
LANES = 128
TURNS = 3
IDS = 8


def iota(shape, dim):
    return lax.broadcasted_iota(jnp.int32, shape, dim)


def hot16(index, *rows):
    found = index == rows[0]
    for row in rows[1:]:
        found = found | (index == row)
    return jnp.where(found, jnp.ones((), BF), jnp.zeros((), BF))


def pack_kernel(owners, cap, rows_dev, tables_hbm, owner_hbm, local_hbm, grad_hbm, own_ref,
                other_ref, turn_ref, tables_ref, owner_ref, local_ref, grad_ref, sems):
    chips = owners // 2
    pairs = (
        (owner_hbm, owner_ref),
        (tables_hbm, tables_ref),
        (local_hbm, local_ref),
        (grad_hbm, grad_ref),
    )
    copies = [pltpu.make_async_copy(a, b, sems.at[i]) for i, (a, b) in enumerate(pairs)]
    for copy in copies:
        copy.start()
    lists, samples = owner_ref.shape
    features = tables_ref.shape[0]
    pool = lists // features
    count = grad_ref.shape[0]
    copies[0].wait()
    owner = owner_ref[...]
    core = lax.axis_index("core")
    owner = owner // 2 + chips * ((owner + core) % 2)

    low = iota((samples, 2 * samples), 0)
    col = iota((samples, 2 * samples), 1)
    tri = jnp.where((low <= col), 1.0, 0.0).astype(BF)
    hot = [iota((owners, samples), 0) == owner[r : r + 1, :] for r in range(lists)]
    stacked = jnp.concatenate([jnp.where(h, 1.0, 0.0) for h in hot], axis=0).astype(BF)
    counts = jnp.dot(stacked, tri, preferred_element_type=F32)
    carry = jnp.zeros((owners, samples), F32)
    places = []
    for r in range(lists):
        block = counts[r * owners : (r + 1) * owners]
        running = block[:, :samples] + carry
        places.append(jnp.sum(jnp.where(hot[r], running, 0.0), axis=0, keepdims=True) - 1.0)
        carry = carry + block[:, samples:]
    place = jnp.concatenate(places, axis=0)

    spread = (iota((samples, count), 1) // features == iota((samples, count), 0))
    spread = jnp.where(spread, 1.0, 0.0).astype(BF)
    both = jnp.concatenate([owner.astype(F32), place], axis=0).astype(BF)
    wide = jnp.dot(both, spread, preferred_element_type=F32)
    slots = []
    lane_f = iota((lists, count), 1) % features
    slot = wide[:lists] * cap + wide[lists:]
    for p in range(pool):
        keep = iota((lists, count), 0) == lane_f * pool + p
        one = jnp.sum(jnp.where(keep, slot, 0.0), axis=0, keepdims=True)
        slots.append(jnp.broadcast_to(one, (16, count)).astype(jnp.int32).astype(jnp.int16)[0:1])

    group = 8
    rows = group * cap
    index = iota((rows, count), 0).astype(jnp.int16)
    copies[3].wait()
    grad = grad_ref[...]
    for g in range(owners // group):
        chosen = hot16(index, *[s - jnp.int16(g * rows) for s in slots])
        picked = jnp.dot(chosen, grad, preferred_element_type=F32)
        picked = picked.astype(BF)
        for k in range(group):
            part = picked[k * cap : (k + 1) * cap]
            out_ref, at = (own_ref, other_ref)[(g * group + k) // chips], (g * group + k) % chips
            out_ref[at, 0:cap, :] = part[:, :LANES]
            out_ref[at, cap : 2 * cap, :] = part[:, LANES:]

    copies[1].wait()
    copies[2].wait()
    table = jnp.zeros((lists, samples), jnp.int32)
    for f in range(features):
        table = jnp.where(iota((lists, samples), 0) // pool == f, tables_ref[f], table)
    target = table * rows_dev + local_ref[...]
    shift = ((lax.axis_index("yx") % 4) * 2 + core) * cap
    lane = place.astype(jnp.int32) + shift
    chunk = lane // LANES
    low_id = (target % 64).astype(F32)
    high_id = (target // 64).astype(F32)
    left, right = [], []
    kind = iota((IDS, samples), 0)
    for r in range(lists):
        row = slice(r, r + 1)
        value = jnp.where(kind < 3, low_id[row], high_id[row])
        value = jnp.where((kind % 3 == chunk[row]) & (kind < 6), value, 0.0)
        blocks = [jnp.where(owner[row] == o, value, 0.0) for o in range(owners)]
        left.append(jnp.concatenate(blocks, axis=0).astype(BF))
        right.append(jnp.where(lane[row] % LANES == iota((LANES, samples), 0), 1.0, 0.0).astype(BF))
    ids = lax.dot_general(
        jnp.concatenate(left, axis=1),
        jnp.concatenate(right, axis=1),
        (((1,), (1,)), ((), ())),
        preferred_element_type=F32,
    )
    ids = ids.reshape(owners, IDS, LANES).astype(BF)
    own_ref[:, 2 * cap : 2 * cap + IDS, :] = ids[:chips]
    other_ref[:, 2 * cap : 2 * cap + IDS, :] = ids[chips:]
    turn_ref[...] = jnp.zeros((IDS, LANES), BF)


def place_kernel(own_ref, out_ref):
    out_ref[...] = own_ref[...]


def merge_kernel(own_ref, got_ref, turn_ref, out_ref, sem):
    rows = own_ref.shape[1] - IDS
    core = lax.axis_index("core")

    def merge(own_at, got_at):
        came = got_ref.at[:, pl.ds(0, rows), :]
        copy = pltpu.make_async_copy(came, out_ref.at[:, pl.ds(got_at, rows), :], sem)
        copy.start()
        out_ref[:, own_at : own_at + rows, :] = own_ref[:, 0:rows, :]
        ids = own_ref[:, rows:, :].astype(F32) + got_ref[:, rows:, :].astype(F32)
        out_ref[:, 2 * rows :, :] = ids.astype(BF)
        turn = jnp.where(iota((IDS, LANES), 0) < 6, ids[0], turn_ref[...].astype(F32))
        out_ref[0, 2 * rows :, :] = turn.astype(BF)
        copy.wait()

    @pl.when(core == 0)
    def _():
        merge(0, rows)

    @pl.when(core == 1)
    def _():
        merge(rows, 0)


def update_kernel(cap, shards, recv_ref, table_ref, state_ref, out_ref):
    chips = recv_ref.shape[0]
    senders = 2 * chips
    rows = table_ref.shape[0]
    part = rows // shards
    ids = recv_ref[:, 4 * cap : 4 * cap + IDS, :].astype(F32)
    ids = jnp.sum(ids.reshape(chips // 4, 4, IDS, LANES), axis=1)
    group = 16
    where, data = [], []
    for g in range(senders // group):
        lanes = []
        for h in range(group // 8):
            x = ids[g * (group // 8) + h]
            lanes += [x[j : j + 1] + 64.0 * x[j + 3 : j + 4] for j in range(3)]
        one = jnp.concatenate(lanes, axis=1)
        one = jnp.broadcast_to(one, (16, group * cap)).astype(jnp.int32).astype(jnp.int16)
        where.append(one[0:1])
        block = recv_ref[g * group // 2 : (g + 1) * group // 2, 0 : 4 * cap, :]
        block = block.reshape(group, 2 * cap, LANES)
        halves = [
            block[:, h * cap : (h + 1) * cap, :].reshape(group * cap, LANES) for h in range(2)
        ]
        data.append(jnp.concatenate(halves, axis=1))
    state = jnp.transpose(state_ref[...])
    index = iota((part, group * cap), 0).astype(jnp.int16)
    spread = []
    for k in range(shards):
        total = jnp.zeros((part, 2 * LANES), F32)
        for g in range(senders // group):
            hot = hot16(index, where[g] - jnp.int16(k * part))
            total = total + jnp.dot(hot, data[g], preferred_element_type=F32)
        square = jnp.sum(total * total, axis=1, keepdims=True) * (1.0 / (2 * LANES))
        columns = []
        for b in range(part // LANES):
            at = k * (part // LANES) + b
            columns.append(state[:, at : at + 1] + square[b * LANES : (b + 1) * LANES])
        new = jnp.concatenate(columns, axis=0)
        old = table_ref[k * part : (k + 1) * part, :].astype(F32)
        out_ref[k, 0:part, :] = (old - 0.3 * total / jnp.sqrt(new)).astype(BF)
        wide = [jnp.transpose(jnp.broadcast_to(c, (LANES, LANES)))[0:1] for c in columns]
        spread.append(jnp.concatenate(wide, axis=1))
    whole = jnp.concatenate(spread, axis=0)
    high = whole.astype(BF).astype(F32)
    both = jnp.concatenate([high, whole - high], axis=0).astype(BF)
    for k in range(shards):
        out_ref[k, part : part + 2 * shards, :] = both


def average_kernel(got_ref, out_ref, state_ref):
    replicas, rows, embed = got_ref.shape
    part = rows - 2 * replicas
    total = got_ref[0].astype(F32)
    for r in range(1, replicas):
        total = total + got_ref[r].astype(F32)
    total = total * (1.0 / replicas)
    table = total[:part].astype(BF)
    for r in range(replicas):
        out_ref[r, :, :] = table
    state = total[part : part + replicas] + total[part + replicas :]
    wide = state_ref.shape[1] // embed
    for k in range(replicas):
        at = (k % wide) * embed
        state_ref[k // wide : k // wide + 1, at : at + embed] = state[k : k + 1]


ALL_VMEM = pltpu.CompilerParams(vmem_limit_bytes=60 * 2**20)
PARAMS = pltpu.CompilerParams(vmem_limit_bytes=32 * 2**20)
VMEM = pl.BlockSpec(memory_space=pltpu.VMEM)
ANY = pl.BlockSpec(memory_space=pl.ANY)


def shards_fn(pooled_grad, owner_ids, local_ids, feature_table, table_rows, adagrad_state):
    samples, features, embed = pooled_grad.shape
    pool = local_ids.shape[2]
    tables, rows_dev = adagrad_state.shape
    chips = lax.axis_size("yx")
    owners = 2 * chips
    replicas = lax.axis_size("rep")
    slots = tables * rows_dev
    count = samples * features * pool
    cap = 3 * count // (2 * owners)
    part = slots // replicas
    owner = jnp.transpose(owner_ids[..., 0], (1, 2, 0)).reshape(features * pool, samples)
    local = jnp.transpose(local_ids, (1, 2, 0)).reshape(features * pool, samples)
    own, other, turn = pl.pallas_call(
        lambda *refs: pack_kernel(owners, cap, rows_dev, *refs),
        out_shape=(
            jax.ShapeDtypeStruct((chips, 2 * cap + IDS, LANES), BF),
            jax.ShapeDtypeStruct((chips, 2 * cap + IDS, LANES), BF),
            jax.ShapeDtypeStruct((IDS, LANES), BF),
        ),
        in_specs=[ANY, ANY, ANY, ANY],
        out_specs=(VMEM, VMEM, VMEM),
        scratch_shapes=[
            pltpu.SMEM((features,), jnp.int32),
            pltpu.VMEM((features * pool, samples), jnp.int32),
            pltpu.VMEM((features * pool, samples), jnp.int32),
            pltpu.VMEM((samples * features, embed), BF),
            pltpu.SemaphoreType.DMA((4,)),
        ],
        compiler_params=ALL_VMEM,
        name="pack",
    )(feature_table, owner, local, pooled_grad.reshape(samples * features, embed))
    got = lax.ppermute(other, "core", [(0, 1), (1, 0)])
    for _ in range(TURNS):
        neighbours = [(2 * i + 1, 2 * (i ^ 1) + 1) for i in range(chips)]
        turn = lax.ppermute(turn, ("yx", "core"), neighbours)
    placed = pl.pallas_call(
        place_kernel,
        out_shape=jax.ShapeDtypeStruct(own.shape, BF),
        in_specs=[VMEM],
        out_specs=VMEM,
        compiler_params=PARAMS,
        name="place",
    )(own)
    send = pl.pallas_call(
        merge_kernel,
        out_shape=jax.ShapeDtypeStruct((chips, 4 * cap + IDS, LANES), BF),
        in_specs=[VMEM, VMEM, VMEM],
        out_specs=VMEM,
        scratch_shapes=[pltpu.SemaphoreType.DMA],
        compiler_params=PARAMS,
        name="merge",
    )(placed, got, turn)
    received = lax.all_to_all(send, "yx", split_axis=0, concat_axis=0, tiled=True)
    updated = pl.pallas_call(
        lambda *refs: update_kernel(cap, replicas, *refs),
        out_shape=jax.ShapeDtypeStruct((replicas, part + 2 * replicas, embed), BF),
        in_specs=[VMEM, VMEM, VMEM],
        out_specs=VMEM,
        compiler_params=PARAMS,
        name="update",
    )(received, table_rows.reshape(slots, embed), adagrad_state.reshape(slots // LANES, LANES))
    mine = lax.all_to_all(updated, "rep", split_axis=0, concat_axis=0, tiled=True)
    copies, state = pl.pallas_call(
        average_kernel,
        out_shape=(
            jax.ShapeDtypeStruct((replicas, part, embed), BF),
            jax.ShapeDtypeStruct((tables, rows_dev), F32),
        ),
        in_specs=[VMEM],
        out_specs=(VMEM, VMEM),
        compiler_params=PARAMS,
        name="average",
    )(mine)
    full = lax.all_to_all(copies, "rep", split_axis=0, concat_axis=0, tiled=True)
    return full.reshape(tables, rows_dev, embed), state


def solution(mesh):
    replicas, owners = mesh.devices.shape
    cores = mesh.devices.reshape(replicas, owners // 2, 2)
    by_core = jax.sharding.Mesh(cores, ("rep", "yx", "core"))
    every, mine = ("rep", "yx", "core"), ("yx", "core")
    placed = (
        P(every, None, None),
        P(every, None, None, None),
        P(every, None, None),
        P(),
        P(None, mine, None),
        P(None, mine),
    )
    return jax.shard_map(
        shards_fn,
        mesh=by_core,
        in_specs=placed,
        out_specs=(P(None, mine, None), P(None, mine)),
        check_vma=False,
    )
```

```python
import jax
import jax.numpy as jnp
from jax import lax
from jax.experimental import pallas as pl
from jax.experimental.pallas import tpu as pltpu
from jax.sharding import PartitionSpec as P

BF = jnp.bfloat16
F32 = jnp.float32
LANES = 128
STEPS = ("next", "next", "near")
IDS = 8


def iota(shape, dim):
    return lax.broadcasted_iota(jnp.int32, shape, dim)


def hot16(index, *rows):
    found = index == rows[0]
    for row in rows[1:]:
        found = found | (index == row)
    return jnp.where(found, jnp.ones((), BF), jnp.zeros((), BF))


def pack_kernel(owners, cap, rows_dev, tables_hbm, owner_hbm, local_hbm, grad_hbm, own_ref,
                other_ref, turn_ref, tables_ref, owner_ref, local_ref, grad_ref, sems):
    chips = owners // 2
    pairs = (
        (owner_hbm, owner_ref),
        (tables_hbm, tables_ref),
        (local_hbm, local_ref),
        (grad_hbm, grad_ref),
    )
    copies = [pltpu.make_async_copy(a, b, sems.at[i]) for i, (a, b) in enumerate(pairs)]
    for copy in copies:
        copy.start()
    lists, samples = owner_ref.shape
    features = tables_ref.shape[0]
    pool = lists // features
    count = grad_ref.shape[0]
    copies[0].wait()
    owner = owner_ref[...]
    core = lax.axis_index("core")
    owner = owner // 2 + chips * ((owner + core) % 2)

    low = iota((samples, 2 * samples), 0)
    col = iota((samples, 2 * samples), 1)
    tri = jnp.where((low <= col), 1.0, 0.0).astype(BF)
    hot = [iota((owners, samples), 0) == owner[r : r + 1, :] for r in range(lists)]
    stacked = jnp.concatenate([jnp.where(h, 1.0, 0.0) for h in hot], axis=0).astype(BF)
    counts = jnp.dot(stacked, tri, preferred_element_type=F32)
    carry = jnp.zeros((owners, samples), F32)
    places = []
    for r in range(lists):
        block = counts[r * owners : (r + 1) * owners]
        running = block[:, :samples] + carry
        places.append(jnp.sum(jnp.where(hot[r], running, 0.0), axis=0, keepdims=True) - 1.0)
        carry = carry + block[:, samples:]
    place = jnp.concatenate(places, axis=0)

    spread = (iota((samples, count), 1) // features == iota((samples, count), 0))
    spread = jnp.where(spread, 1.0, 0.0).astype(BF)
    both = jnp.concatenate([owner.astype(F32), place], axis=0).astype(BF)
    wide = jnp.dot(both, spread, preferred_element_type=F32)
    slots = []
    lane_f = iota((lists, count), 1) % features
    slot = wide[:lists] * cap + wide[lists:]
    for p in range(pool):
        keep = iota((lists, count), 0) == lane_f * pool + p
        one = jnp.sum(jnp.where(keep, slot, 0.0), axis=0, keepdims=True)
        slots.append(jnp.broadcast_to(one, (16, count)).astype(jnp.int32).astype(jnp.int16)[0:1])

    group = 8
    rows = group * cap
    index = iota((rows, count), 0).astype(jnp.int16)
    copies[3].wait()
    grad = grad_ref[...]
    for g in range(owners // group):
        chosen = hot16(index, *[s - jnp.int16(g * rows) for s in slots])
        picked = jnp.dot(chosen, grad, preferred_element_type=F32)
        picked = picked.astype(BF)
        for k in range(group):
            part = picked[k * cap : (k + 1) * cap]
            out_ref, at = (own_ref, other_ref)[(g * group + k) // chips], (g * group + k) % chips
            out_ref[at, 0:cap, :] = part[:, :LANES]
            out_ref[at, cap : 2 * cap, :] = part[:, LANES:]

    copies[1].wait()
    copies[2].wait()
    table = jnp.zeros((lists, samples), jnp.int32)
    for f in range(features):
        table = jnp.where(iota((lists, samples), 0) // pool == f, tables_ref[f], table)
    target = table * rows_dev + local_ref[...]
    shift = ((lax.axis_index("yx") % 4) * 2 + core) * cap
    lane = place.astype(jnp.int32) + shift
    chunk = lane // LANES
    low_id = (target % 64).astype(F32)
    high_id = (target // 64).astype(F32)
    left, right = [], []
    kind = iota((IDS, samples), 0)
    for r in range(lists):
        row = slice(r, r + 1)
        value = jnp.where(kind < 3, low_id[row], high_id[row])
        value = jnp.where((kind % 3 == chunk[row]) & (kind < 6), value, 0.0)
        blocks = [jnp.where(owner[row] == o, value, 0.0) for o in range(owners)]
        left.append(jnp.concatenate(blocks, axis=0).astype(BF))
        right.append(jnp.where(lane[row] % LANES == iota((LANES, samples), 0), 1.0, 0.0).astype(BF))
    ids = lax.dot_general(
        jnp.concatenate(left, axis=1),
        jnp.concatenate(right, axis=1),
        (((1,), (1,)), ((), ())),
        preferred_element_type=F32,
    )
    ids = ids.reshape(owners, IDS, LANES).astype(BF)
    own_ref[:, 2 * cap : 2 * cap + IDS, :] = ids[:chips]
    other_ref[:, 2 * cap : 2 * cap + IDS, :] = ids[chips:]
    turn_ref[...] = jnp.zeros((IDS, LANES), BF)


def place_kernel(own_ref, out_ref):
    out_ref[...] = own_ref[...]


def merge_kernel(own_ref, got_ref, turn_ref, out_ref, sem):
    rows = own_ref.shape[1] - IDS
    core = lax.axis_index("core")

    def merge(own_at, got_at):
        came = got_ref.at[:, pl.ds(0, rows), :]
        copy = pltpu.make_async_copy(came, out_ref.at[:, pl.ds(got_at, rows), :], sem)
        copy.start()
        out_ref[:, own_at : own_at + rows, :] = own_ref[:, 0:rows, :]
        ids = own_ref[:, rows:, :].astype(F32) + got_ref[:, rows:, :].astype(F32)
        out_ref[:, 2 * rows :, :] = ids.astype(BF)
        turn = jnp.where(iota((IDS, LANES), 0) < 6, ids[0], turn_ref[...].astype(F32))
        out_ref[0, 2 * rows :, :] = turn.astype(BF)
        copy.wait()

    @pl.when(core == 0)
    def _():
        merge(0, rows)

    @pl.when(core == 1)
    def _():
        merge(rows, 0)


def update_kernel(cap, shards, recv_ref, table_ref, state_ref, out_ref):
    chips = recv_ref.shape[0]
    senders = 2 * chips
    rows = table_ref.shape[0]
    part = rows // shards
    ids = recv_ref[:, 4 * cap : 4 * cap + IDS, :].astype(F32)
    ids = jnp.sum(ids.reshape(chips // 4, 4, IDS, LANES), axis=1)
    group = 16
    where, data = [], []
    for g in range(senders // group):
        lanes = []
        for h in range(group // 8):
            x = ids[g * (group // 8) + h]
            lanes += [x[j : j + 1] + 64.0 * x[j + 3 : j + 4] for j in range(3)]
        one = jnp.concatenate(lanes, axis=1)
        one = jnp.broadcast_to(one, (16, group * cap)).astype(jnp.int32).astype(jnp.int16)
        where.append(one[0:1])
        block = recv_ref[g * group // 2 : (g + 1) * group // 2, 0 : 4 * cap, :]
        block = block.reshape(group, 2 * cap, LANES)
        halves = [
            block[:, h * cap : (h + 1) * cap, :].reshape(group * cap, LANES) for h in range(2)
        ]
        data.append(jnp.concatenate(halves, axis=1))
    state = jnp.transpose(state_ref[...])
    index = iota((part, group * cap), 0).astype(jnp.int16)
    spread = []
    for k in range(shards):
        total = jnp.zeros((part, 2 * LANES), F32)
        for g in range(senders // group):
            hot = hot16(index, where[g] - jnp.int16(k * part))
            total = total + jnp.dot(hot, data[g], preferred_element_type=F32)
        square = jnp.sum(total * total, axis=1, keepdims=True) * (1.0 / (2 * LANES))
        columns = []
        for b in range(part // LANES):
            at = k * (part // LANES) + b
            columns.append(state[:, at : at + 1] + square[b * LANES : (b + 1) * LANES])
        new = jnp.concatenate(columns, axis=0)
        old = table_ref[k * part : (k + 1) * part, :].astype(F32)
        out_ref[k, 0:part, :] = (old - 0.3 * total / jnp.sqrt(new)).astype(BF)
        wide = [jnp.transpose(jnp.broadcast_to(c, (LANES, LANES)))[0:1] for c in columns]
        spread.append(jnp.concatenate(wide, axis=1))
    whole = jnp.concatenate(spread, axis=0)
    high = whole.astype(BF).astype(F32)
    both = jnp.concatenate([high, whole - high], axis=0).astype(BF)
    for k in range(shards):
        out_ref[k, part : part + 2 * shards, :] = both


def average_kernel(got_ref, out_ref, state_ref):
    replicas, rows, embed = got_ref.shape
    part = rows - 2 * replicas
    total = got_ref[0].astype(F32)
    for r in range(1, replicas):
        total = total + got_ref[r].astype(F32)
    total = total * (1.0 / replicas)
    table = total[:part].astype(BF)
    for r in range(replicas):
        out_ref[r, :, :] = table
    state = total[part : part + replicas] + total[part + replicas :]
    wide = state_ref.shape[1] // embed
    for k in range(replicas):
        at = (k % wide) * embed
        state_ref[k // wide : k // wide + 1, at : at + embed] = state[k : k + 1]


ALL_VMEM = pltpu.CompilerParams(vmem_limit_bytes=60 * 2**20)
PARAMS = pltpu.CompilerParams(vmem_limit_bytes=32 * 2**20)
VMEM = pl.BlockSpec(memory_space=pltpu.VMEM)
ANY = pl.BlockSpec(memory_space=pl.ANY)


def shards_fn(pooled_grad, owner_ids, local_ids, feature_table, table_rows, adagrad_state):
    samples, features, embed = pooled_grad.shape
    pool = local_ids.shape[2]
    tables, rows_dev = adagrad_state.shape
    chips = lax.axis_size("yx")
    owners = 2 * chips
    replicas = lax.axis_size("rep")
    slots = tables * rows_dev
    count = samples * features * pool
    cap = 3 * count // (2 * owners)
    part = slots // replicas
    owner = jnp.transpose(owner_ids[..., 0], (1, 2, 0)).reshape(features * pool, samples)
    local = jnp.transpose(local_ids, (1, 2, 0)).reshape(features * pool, samples)
    own, other, turn = pl.pallas_call(
        lambda *refs: pack_kernel(owners, cap, rows_dev, *refs),
        out_shape=(
            jax.ShapeDtypeStruct((chips, 2 * cap + IDS, LANES), BF),
            jax.ShapeDtypeStruct((chips, 2 * cap + IDS, LANES), BF),
            jax.ShapeDtypeStruct((IDS, LANES), BF),
        ),
        in_specs=[ANY, ANY, ANY, ANY],
        out_specs=(VMEM, VMEM, VMEM),
        scratch_shapes=[
            pltpu.SMEM((features,), jnp.int32),
            pltpu.VMEM((features * pool, samples), jnp.int32),
            pltpu.VMEM((features * pool, samples), jnp.int32),
            pltpu.VMEM((samples * features, embed), BF),
            pltpu.SemaphoreType.DMA((4,)),
        ],
        compiler_params=ALL_VMEM,
        name="pack",
    )(feature_table, owner, local, pooled_grad.reshape(samples * features, embed))
    got = lax.ppermute(other, "core", [(0, 1), (1, 0)])
    for step in STEPS:
        to = [(i + 1) % chips if step == "next" else i ^ 1 for i in range(chips)]
        turn = lax.ppermute(turn, ("yx", "core"), [(2 * i + 1, 2 * to[i] + 1) for i in range(chips)])
    placed = pl.pallas_call(
        place_kernel,
        out_shape=jax.ShapeDtypeStruct(own.shape, BF),
        in_specs=[VMEM],
        out_specs=VMEM,
        compiler_params=PARAMS,
        name="place",
    )(own)
    send = pl.pallas_call(
        merge_kernel,
        out_shape=jax.ShapeDtypeStruct((chips, 4 * cap + IDS, LANES), BF),
        in_specs=[VMEM, VMEM, VMEM],
        out_specs=VMEM,
        scratch_shapes=[pltpu.SemaphoreType.DMA],
        compiler_params=PARAMS,
        name="merge",
    )(placed, got, turn)
    received = lax.all_to_all(send, "yx", split_axis=0, concat_axis=0, tiled=True)
    updated = pl.pallas_call(
        lambda *refs: update_kernel(cap, replicas, *refs),
        out_shape=jax.ShapeDtypeStruct((replicas, part + 2 * replicas, embed), BF),
        in_specs=[VMEM, VMEM, VMEM],
        out_specs=VMEM,
        compiler_params=PARAMS,
        name="update",
    )(received, table_rows.reshape(slots, embed), adagrad_state.reshape(slots // LANES, LANES))
    mine = lax.all_to_all(updated, "rep", split_axis=0, concat_axis=0, tiled=True)
    copies, state = pl.pallas_call(
        average_kernel,
        out_shape=(
            jax.ShapeDtypeStruct((replicas, part, embed), BF),
            jax.ShapeDtypeStruct((tables, rows_dev), F32),
        ),
        in_specs=[VMEM],
        out_specs=(VMEM, VMEM),
        compiler_params=PARAMS,
        name="average",
    )(mine)
    full = lax.all_to_all(copies, "rep", split_axis=0, concat_axis=0, tiled=True)
    return full.reshape(tables, rows_dev, embed), state


def solution(mesh):
    replicas, owners = mesh.devices.shape
    cores = mesh.devices.reshape(replicas, owners // 2, 2)
    by_core = jax.sharding.Mesh(cores, ("rep", "yx", "core"))
    every, mine = ("rep", "yx", "core"), ("yx", "core")
    placed = (
        P(every, None, None),
        P(every, None, None, None),
        P(every, None, None),
        P(),
        P(None, mine, None),
        P(None, mine),
    )
    return jax.shard_map(
        shards_fn,
        mesh=by_core,
        in_specs=placed,
        out_specs=(P(None, mine, None), P(None, mine)),
        check_vma=False,
    )
```

```python
import jax
import jax.numpy as jnp
from jax import lax
from jax.experimental import pallas as pl
from jax.experimental.pallas import tpu as pltpu
from jax.sharding import PartitionSpec as P

BF = jnp.bfloat16
F32 = jnp.float32
LANES = 128
STEPS = ("next", "next", "near", "near")
IDS = 8


def iota(shape, dim):
    return lax.broadcasted_iota(jnp.int32, shape, dim)


def hot16(index, *rows):
    found = index == rows[0]
    for row in rows[1:]:
        found = found | (index == row)
    return jnp.where(found, jnp.ones((), BF), jnp.zeros((), BF))


def pack_kernel(owners, cap, rows_dev, tables_hbm, owner_hbm, local_hbm, grad_hbm, own_ref,
                other_ref, turn_ref, tables_ref, owner_ref, local_ref, grad_ref, sems):
    chips = owners // 2
    pairs = (
        (owner_hbm, owner_ref),
        (tables_hbm, tables_ref),
        (local_hbm, local_ref),
        (grad_hbm, grad_ref),
    )
    copies = [pltpu.make_async_copy(a, b, sems.at[i]) for i, (a, b) in enumerate(pairs)]
    for copy in copies:
        copy.start()
    lists, samples = owner_ref.shape
    features = tables_ref.shape[0]
    pool = lists // features
    count = grad_ref.shape[0]
    copies[0].wait()
    owner = owner_ref[...]
    core = lax.axis_index("core")
    owner = owner // 2 + chips * ((owner + core) % 2)

    low = iota((samples, 2 * samples), 0)
    col = iota((samples, 2 * samples), 1)
    tri = jnp.where((low <= col), 1.0, 0.0).astype(BF)
    hot = [iota((owners, samples), 0) == owner[r : r + 1, :] for r in range(lists)]
    stacked = jnp.concatenate([jnp.where(h, 1.0, 0.0) for h in hot], axis=0).astype(BF)
    counts = jnp.dot(stacked, tri, preferred_element_type=F32)
    carry = jnp.zeros((owners, samples), F32)
    places = []
    for r in range(lists):
        block = counts[r * owners : (r + 1) * owners]
        running = block[:, :samples] + carry
        places.append(jnp.sum(jnp.where(hot[r], running, 0.0), axis=0, keepdims=True) - 1.0)
        carry = carry + block[:, samples:]
    place = jnp.concatenate(places, axis=0)

    spread = (iota((samples, count), 1) // features == iota((samples, count), 0))
    spread = jnp.where(spread, 1.0, 0.0).astype(BF)
    both = jnp.concatenate([owner.astype(F32), place], axis=0).astype(BF)
    wide = jnp.dot(both, spread, preferred_element_type=F32)
    slots = []
    lane_f = iota((lists, count), 1) % features
    slot = wide[:lists] * cap + wide[lists:]
    for p in range(pool):
        keep = iota((lists, count), 0) == lane_f * pool + p
        one = jnp.sum(jnp.where(keep, slot, 0.0), axis=0, keepdims=True)
        slots.append(jnp.broadcast_to(one, (16, count)).astype(jnp.int32).astype(jnp.int16)[0:1])

    group = 8
    rows = group * cap
    index = iota((rows, count), 0).astype(jnp.int16)
    copies[3].wait()
    grad = grad_ref[...]
    for g in range(owners // group):
        chosen = hot16(index, *[s - jnp.int16(g * rows) for s in slots])
        picked = jnp.dot(chosen, grad, preferred_element_type=F32)
        picked = picked.astype(BF)
        for k in range(group):
            part = picked[k * cap : (k + 1) * cap]
            out_ref, at = (own_ref, other_ref)[(g * group + k) // chips], (g * group + k) % chips
            out_ref[at, 0:cap, :] = part[:, :LANES]
            out_ref[at, cap : 2 * cap, :] = part[:, LANES:]

    copies[1].wait()
    copies[2].wait()
    table = jnp.zeros((lists, samples), jnp.int32)
    for f in range(features):
        table = jnp.where(iota((lists, samples), 0) // pool == f, tables_ref[f], table)
    target = table * rows_dev + local_ref[...]
    shift = ((lax.axis_index("yx") % 4) * 2 + core) * cap
    lane = place.astype(jnp.int32) + shift
    chunk = lane // LANES
    low_id = (target % 64).astype(F32)
    high_id = (target // 64).astype(F32)
    left, right = [], []
    kind = iota((IDS, samples), 0)
    for r in range(lists):
        row = slice(r, r + 1)
        value = jnp.where(kind < 3, low_id[row], high_id[row])
        value = jnp.where((kind % 3 == chunk[row]) & (kind < 6), value, 0.0)
        blocks = [jnp.where(owner[row] == o, value, 0.0) for o in range(owners)]
        left.append(jnp.concatenate(blocks, axis=0).astype(BF))
        right.append(jnp.where(lane[row] % LANES == iota((LANES, samples), 0), 1.0, 0.0).astype(BF))
    ids = lax.dot_general(
        jnp.concatenate(left, axis=1),
        jnp.concatenate(right, axis=1),
        (((1,), (1,)), ((), ())),
        preferred_element_type=F32,
    )
    ids = ids.reshape(owners, IDS, LANES).astype(BF)
    own_ref[:, 2 * cap : 2 * cap + IDS, :] = ids[:chips]
    other_ref[:, 2 * cap : 2 * cap + IDS, :] = ids[chips:]
    turn_ref[...] = jnp.zeros((IDS, LANES), BF)


def place_kernel(own_ref, out_ref):
    out_ref[...] = own_ref[...]


def merge_kernel(own_ref, got_ref, turn_ref, out_ref, sem):
    rows = own_ref.shape[1] - IDS
    core = lax.axis_index("core")

    def merge(own_at, got_at):
        came = got_ref.at[:, pl.ds(0, rows), :]
        copy = pltpu.make_async_copy(came, out_ref.at[:, pl.ds(got_at, rows), :], sem)
        copy.start()
        out_ref[:, own_at : own_at + rows, :] = own_ref[:, 0:rows, :]
        ids = own_ref[:, rows:, :].astype(F32) + got_ref[:, rows:, :].astype(F32)
        out_ref[:, 2 * rows :, :] = ids.astype(BF)
        turn = jnp.where(iota((IDS, LANES), 0) < 6, ids[0], turn_ref[...].astype(F32))
        out_ref[0, 2 * rows :, :] = turn.astype(BF)
        copy.wait()

    @pl.when(core == 0)
    def _():
        merge(0, rows)

    @pl.when(core == 1)
    def _():
        merge(rows, 0)


def update_kernel(cap, shards, recv_ref, table_ref, state_ref, out_ref):
    chips = recv_ref.shape[0]
    senders = 2 * chips
    rows = table_ref.shape[0]
    part = rows // shards
    ids = recv_ref[:, 4 * cap : 4 * cap + IDS, :].astype(F32)
    ids = jnp.sum(ids.reshape(chips // 4, 4, IDS, LANES), axis=1)
    group = 16
    where, data = [], []
    for g in range(senders // group):
        lanes = []
        for h in range(group // 8):
            x = ids[g * (group // 8) + h]
            lanes += [x[j : j + 1] + 64.0 * x[j + 3 : j + 4] for j in range(3)]
        one = jnp.concatenate(lanes, axis=1)
        one = jnp.broadcast_to(one, (16, group * cap)).astype(jnp.int32).astype(jnp.int16)
        where.append(one[0:1])
        block = recv_ref[g * group // 2 : (g + 1) * group // 2, 0 : 4 * cap, :]
        block = block.reshape(group, 2 * cap, LANES)
        halves = [
            block[:, h * cap : (h + 1) * cap, :].reshape(group * cap, LANES) for h in range(2)
        ]
        data.append(jnp.concatenate(halves, axis=1))
    state = jnp.transpose(state_ref[...])
    index = iota((part, group * cap), 0).astype(jnp.int16)
    spread = []
    for k in range(shards):
        total = jnp.zeros((part, 2 * LANES), F32)
        for g in range(senders // group):
            hot = hot16(index, where[g] - jnp.int16(k * part))
            total = total + jnp.dot(hot, data[g], preferred_element_type=F32)
        square = jnp.sum(total * total, axis=1, keepdims=True) * (1.0 / (2 * LANES))
        columns = []
        for b in range(part // LANES):
            at = k * (part // LANES) + b
            columns.append(state[:, at : at + 1] + square[b * LANES : (b + 1) * LANES])
        new = jnp.concatenate(columns, axis=0)
        old = table_ref[k * part : (k + 1) * part, :].astype(F32)
        out_ref[k, 0:part, :] = (old - 0.3 * total / jnp.sqrt(new)).astype(BF)
        wide = [jnp.transpose(jnp.broadcast_to(c, (LANES, LANES)))[0:1] for c in columns]
        spread.append(jnp.concatenate(wide, axis=1))
    whole = jnp.concatenate(spread, axis=0)
    high = whole.astype(BF).astype(F32)
    both = jnp.concatenate([high, whole - high], axis=0).astype(BF)
    for k in range(shards):
        out_ref[k, part : part + 2 * shards, :] = both


def average_kernel(got_ref, out_ref, state_ref):
    replicas, rows, embed = got_ref.shape
    part = rows - 2 * replicas
    total = got_ref[0].astype(F32)
    for r in range(1, replicas):
        total = total + got_ref[r].astype(F32)
    total = total * (1.0 / replicas)
    table = total[:part].astype(BF)
    for r in range(replicas):
        out_ref[r, :, :] = table
    state = total[part : part + replicas] + total[part + replicas :]
    wide = state_ref.shape[1] // embed
    for k in range(replicas):
        at = (k % wide) * embed
        state_ref[k // wide : k // wide + 1, at : at + embed] = state[k : k + 1]


ALL_VMEM = pltpu.CompilerParams(vmem_limit_bytes=60 * 2**20)
PARAMS = pltpu.CompilerParams(vmem_limit_bytes=32 * 2**20)
VMEM = pl.BlockSpec(memory_space=pltpu.VMEM)
ANY = pl.BlockSpec(memory_space=pl.ANY)


def shards_fn(pooled_grad, owner_ids, local_ids, feature_table, table_rows, adagrad_state):
    samples, features, embed = pooled_grad.shape
    pool = local_ids.shape[2]
    tables, rows_dev = adagrad_state.shape
    chips = lax.axis_size("yx")
    owners = 2 * chips
    replicas = lax.axis_size("rep")
    slots = tables * rows_dev
    count = samples * features * pool
    cap = 3 * count // (2 * owners)
    part = slots // replicas
    owner = jnp.transpose(owner_ids[..., 0], (1, 2, 0)).reshape(features * pool, samples)
    local = jnp.transpose(local_ids, (1, 2, 0)).reshape(features * pool, samples)
    own, other, turn = pl.pallas_call(
        lambda *refs: pack_kernel(owners, cap, rows_dev, *refs),
        out_shape=(
            jax.ShapeDtypeStruct((chips, 2 * cap + IDS, LANES), BF),
            jax.ShapeDtypeStruct((chips, 2 * cap + IDS, LANES), BF),
            jax.ShapeDtypeStruct((IDS, LANES), BF),
        ),
        in_specs=[ANY, ANY, ANY, ANY],
        out_specs=(VMEM, VMEM, VMEM),
        scratch_shapes=[
            pltpu.SMEM((features,), jnp.int32),
            pltpu.VMEM((features * pool, samples), jnp.int32),
            pltpu.VMEM((features * pool, samples), jnp.int32),
            pltpu.VMEM((samples * features, embed), BF),
            pltpu.SemaphoreType.DMA((4,)),
        ],
        compiler_params=ALL_VMEM,
        name="pack",
    )(feature_table, owner, local, pooled_grad.reshape(samples * features, embed))
    got = lax.ppermute(other, "core", [(0, 1), (1, 0)])
    for step in STEPS:
        to = [(i + 1) % chips if step == "next" else i ^ 1 for i in range(chips)]
        turn = lax.ppermute(turn, ("yx", "core"), [(2 * i + 1, 2 * to[i] + 1) for i in range(chips)])
    placed = pl.pallas_call(
        place_kernel,
        out_shape=jax.ShapeDtypeStruct(own.shape, BF),
        in_specs=[VMEM],
        out_specs=VMEM,
        compiler_params=PARAMS,
        name="place",
    )(own)
    send = pl.pallas_call(
        merge_kernel,
        out_shape=jax.ShapeDtypeStruct((chips, 4 * cap + IDS, LANES), BF),
        in_specs=[VMEM, VMEM, VMEM],
        out_specs=VMEM,
        scratch_shapes=[pltpu.SemaphoreType.DMA],
        compiler_params=PARAMS,
        name="merge",
    )(placed, got, turn)
    received = lax.all_to_all(send, "yx", split_axis=0, concat_axis=0, tiled=True)
    updated = pl.pallas_call(
        lambda *refs: update_kernel(cap, replicas, *refs),
        out_shape=jax.ShapeDtypeStruct((replicas, part + 2 * replicas, embed), BF),
        in_specs=[VMEM, VMEM, VMEM],
        out_specs=VMEM,
        compiler_params=PARAMS,
        name="update",
    )(received, table_rows.reshape(slots, embed), adagrad_state.reshape(slots // LANES, LANES))
    mine = lax.all_to_all(updated, "rep", split_axis=0, concat_axis=0, tiled=True)
    copies, state = pl.pallas_call(
        average_kernel,
        out_shape=(
            jax.ShapeDtypeStruct((replicas, part, embed), BF),
            jax.ShapeDtypeStruct((tables, rows_dev), F32),
        ),
        in_specs=[VMEM],
        out_specs=(VMEM, VMEM),
        compiler_params=PARAMS,
        name="average",
    )(mine)
    full = lax.all_to_all(copies, "rep", split_axis=0, concat_axis=0, tiled=True)
    return full.reshape(tables, rows_dev, embed), state


def solution(mesh):
    replicas, owners = mesh.devices.shape
    cores = mesh.devices.reshape(replicas, owners // 2, 2)
    by_core = jax.sharding.Mesh(cores, ("rep", "yx", "core"))
    every, mine = ("rep", "yx", "core"), ("yx", "core")
    placed = (
        P(every, None, None),
        P(every, None, None, None),
        P(every, None, None),
        P(),
        P(None, mine, None),
        P(None, mine),
    )
    return jax.shard_map(
        shards_fn,
        mesh=by_core,
        in_specs=placed,
        out_specs=(P(None, mine, None), P(None, mine)),
        check_vma=False,
    )
```

```python
import jax
import jax.numpy as jnp
from jax import lax
from jax.experimental import pallas as pl
from jax.experimental.pallas import tpu as pltpu
from jax.sharding import PartitionSpec as P

BF = jnp.bfloat16
F32 = jnp.float32
LANES = 128
STEPS = ("next", "next", "near")
IDS = 8


def iota(shape, dim):
    return lax.broadcasted_iota(jnp.int32, shape, dim)


def hot16(index, *rows):
    found = index == rows[0]
    for row in rows[1:]:
        found = found | (index == row)
    return jnp.where(found, jnp.ones((), BF), jnp.zeros((), BF))


def pack_kernel(owners, cap, rows_dev, tables_hbm, owner_hbm, local_hbm, grad_hbm, own_ref,
                other_ref, turn_ref, tables_ref, owner_ref, local_ref, grad_ref, sems):
    chips = owners // 2
    pairs = (
        (owner_hbm, owner_ref),
        (tables_hbm, tables_ref),
        (local_hbm, local_ref),
        (grad_hbm, grad_ref),
    )
    copies = [pltpu.make_async_copy(a, b, sems.at[i]) for i, (a, b) in enumerate(pairs)]
    for copy in copies:
        copy.start()
    lists, samples = owner_ref.shape
    features = tables_ref.shape[0]
    pool = lists // features
    count = grad_ref.shape[0]
    copies[0].wait()
    owner = owner_ref[...]
    core = lax.axis_index("core")
    owner = owner // 2 + chips * ((owner + core) % 2)

    low = iota((samples, 2 * samples), 0)
    col = iota((samples, 2 * samples), 1)
    tri = jnp.where((low <= col), 1.0, 0.0).astype(BF)
    hot = [iota((owners, samples), 0) == owner[r : r + 1, :] for r in range(lists)]
    stacked = jnp.concatenate([jnp.where(h, 1.0, 0.0) for h in hot], axis=0).astype(BF)
    counts = jnp.dot(stacked, tri, preferred_element_type=F32)
    carry = jnp.zeros((owners, samples), F32)
    places = []
    for r in range(lists):
        block = counts[r * owners : (r + 1) * owners]
        running = block[:, :samples] + carry
        places.append(jnp.sum(jnp.where(hot[r], running, 0.0), axis=0, keepdims=True) - 1.0)
        carry = carry + block[:, samples:]
    place = jnp.concatenate(places, axis=0)

    spread = (iota((samples, count), 1) // features == iota((samples, count), 0))
    spread = jnp.where(spread, 1.0, 0.0).astype(BF)
    both = jnp.concatenate([owner.astype(F32), place], axis=0).astype(BF)
    wide = jnp.dot(both, spread, preferred_element_type=F32)
    slots = []
    lane_f = iota((lists, count), 1) % features
    slot = wide[:lists] * cap + wide[lists:]
    for p in range(pool):
        keep = iota((lists, count), 0) == lane_f * pool + p
        one = jnp.sum(jnp.where(keep, slot, 0.0), axis=0, keepdims=True)
        slots.append(jnp.broadcast_to(one, (16, count)).astype(jnp.int32).astype(jnp.int16)[0:1])

    group = 8
    rows = group * cap
    index = iota((rows, count), 0).astype(jnp.int16)
    copies[3].wait()
    grad = grad_ref[...]
    for g in range(owners // group):
        chosen = hot16(index, *[s - jnp.int16(g * rows) for s in slots])
        picked = jnp.dot(chosen, grad, preferred_element_type=F32)
        picked = picked.astype(BF)
        for k in range(group):
            part = picked[k * cap : (k + 1) * cap]
            out_ref, at = (own_ref, other_ref)[(g * group + k) // chips], (g * group + k) % chips
            out_ref[at, 0:cap, :] = part[:, :LANES]
            out_ref[at, cap : 2 * cap, :] = part[:, LANES:]

    copies[1].wait()
    copies[2].wait()
    table = jnp.zeros((lists, samples), jnp.int32)
    for f in range(features):
        table = jnp.where(iota((lists, samples), 0) // pool == f, tables_ref[f], table)
    target = table * rows_dev + local_ref[...]
    shift = ((lax.axis_index("yx") % 4) * 2 + core) * cap
    lane = place.astype(jnp.int32) + shift
    chunk = lane // LANES
    low_id = (target % 64).astype(F32)
    high_id = (target // 64).astype(F32)
    left, right = [], []
    kind = iota((IDS, samples), 0)
    for r in range(lists):
        row = slice(r, r + 1)
        value = jnp.where(kind < 3, low_id[row], high_id[row])
        value = jnp.where((kind % 3 == chunk[row]) & (kind < 6), value, 0.0)
        blocks = [jnp.where(owner[row] == o, value, 0.0) for o in range(owners)]
        left.append(jnp.concatenate(blocks, axis=0).astype(BF))
        right.append(jnp.where(lane[row] % LANES == iota((LANES, samples), 0), 1.0, 0.0).astype(BF))
    ids = lax.dot_general(
        jnp.concatenate(left, axis=1),
        jnp.concatenate(right, axis=1),
        (((1,), (1,)), ((), ())),
        preferred_element_type=F32,
    )
    ids = ids.reshape(owners, IDS, LANES).astype(BF)
    own_ref[:, 2 * cap : 2 * cap + IDS, :] = ids[:chips]
    other_ref[:, 2 * cap : 2 * cap + IDS, :] = ids[chips:]
    turn_ref[...] = jnp.zeros((IDS, LANES), BF)


def place_kernel(own_ref, out_ref):
    out_ref[...] = own_ref[...]


def merge_kernel(own_ref, got_ref, turn_ref, out_ref, sem):
    rows = own_ref.shape[1] - IDS
    core = lax.axis_index("core")

    def merge(own_at, got_at):
        came = got_ref.at[:, pl.ds(0, rows), :]
        copy = pltpu.make_async_copy(came, out_ref.at[:, pl.ds(got_at, rows), :], sem)
        copy.start()
        out_ref[:, own_at : own_at + rows, :] = own_ref[:, 0:rows, :]
        ids = own_ref[:, rows:, :].astype(F32) + got_ref[:, rows:, :].astype(F32)
        out_ref[:, 2 * rows :, :] = ids.astype(BF)
        turn = jnp.where(iota((IDS, LANES), 0) < 6, ids[0], turn_ref[...].astype(F32))
        out_ref[0, 2 * rows :, :] = turn.astype(BF)
        copy.wait()

    @pl.when(core == 0)
    def _():
        merge(0, rows)

    @pl.when(core == 1)
    def _():
        merge(rows, 0)


def update_kernel(cap, shards, recv_ref, table_ref, state_ref, out_ref):
    chips = recv_ref.shape[0]
    senders = 2 * chips
    rows = table_ref.shape[0]
    part = rows // shards
    ids = recv_ref[:, 4 * cap : 4 * cap + IDS, :].astype(F32)
    ids = jnp.sum(ids.reshape(chips // 4, 4, IDS, LANES), axis=1)
    group = 16
    where, data = [], []
    for g in range(senders // group):
        lanes = []
        for h in range(group // 8):
            x = ids[g * (group // 8) + h]
            lanes += [x[j : j + 1] + 64.0 * x[j + 3 : j + 4] for j in range(3)]
        one = jnp.concatenate(lanes, axis=1)
        one = jnp.broadcast_to(one, (16, group * cap)).astype(jnp.int32).astype(jnp.int16)
        where.append(one[0:1])
        block = recv_ref[g * group // 2 : (g + 1) * group // 2, 0 : 4 * cap, :]
        block = block.reshape(group, 2 * cap, LANES)
        halves = [
            block[:, h * cap : (h + 1) * cap, :].reshape(group * cap, LANES) for h in range(2)
        ]
        data.append(jnp.concatenate(halves, axis=1))
    state = jnp.transpose(state_ref[...])
    index = iota((part, group * cap), 0).astype(jnp.int16)
    spread = []
    for k in range(shards):
        total = jnp.zeros((part, 2 * LANES), F32)
        for g in range(senders // group):
            hot = hot16(index, where[g] - jnp.int16(k * part))
            total = total + jnp.dot(hot, data[g], preferred_element_type=F32)
        square = jnp.sum(total * total, axis=1, keepdims=True) * (1.0 / (2 * LANES))
        columns = []
        for b in range(part // LANES):
            at = k * (part // LANES) + b
            columns.append(state[:, at : at + 1] + square[b * LANES : (b + 1) * LANES])
        new = jnp.concatenate(columns, axis=0)
        old = table_ref[k * part : (k + 1) * part, :].astype(F32)
        out_ref[k, 0:part, :] = (old - 0.3 * total / jnp.sqrt(new)).astype(BF)
        wide = [jnp.transpose(jnp.broadcast_to(c, (LANES, LANES)))[0:1] for c in columns]
        spread.append(jnp.concatenate(wide, axis=1))
    whole = jnp.concatenate(spread, axis=0)
    high = whole.astype(BF).astype(F32)
    both = jnp.concatenate([high, whole - high], axis=0).astype(BF)
    for k in range(shards):
        out_ref[k, part : part + 2 * shards, :] = both


def average_kernel(got_ref, out_ref, state_ref):
    replicas, rows, embed = got_ref.shape
    part = rows - 2 * replicas
    total = got_ref[0].astype(F32)
    for r in range(1, replicas):
        total = total + got_ref[r].astype(F32)
    total = total * (1.0 / replicas)
    table = total[:part].astype(BF)
    for r in range(replicas):
        out_ref[r, :, :] = table
    state = total[part : part + replicas] + total[part + replicas :]
    wide = state_ref.shape[1] // embed
    for k in range(replicas):
        at = (k % wide) * embed
        state_ref[k // wide : k // wide + 1, at : at + embed] = state[k : k + 1]


ALL_VMEM = pltpu.CompilerParams(vmem_limit_bytes=60 * 2**20)
PARAMS = pltpu.CompilerParams(vmem_limit_bytes=32 * 2**20)
VMEM = pl.BlockSpec(memory_space=pltpu.VMEM)
ANY = pl.BlockSpec(memory_space=pl.ANY)


def shards_fn(pooled_grad, owner_ids, local_ids, feature_table, table_rows, adagrad_state):
    samples, features, embed = pooled_grad.shape
    pool = local_ids.shape[2]
    tables, rows_dev = adagrad_state.shape
    chips = lax.axis_size("yx")
    owners = 2 * chips
    replicas = lax.axis_size("rep")
    slots = tables * rows_dev
    count = samples * features * pool
    cap = 3 * count // (2 * owners)
    part = slots // replicas
    owner = jnp.transpose(owner_ids[..., 0], (1, 2, 0)).reshape(features * pool, samples)
    local = jnp.transpose(local_ids, (1, 2, 0)).reshape(features * pool, samples)
    own, other, turn = pl.pallas_call(
        lambda *refs: pack_kernel(owners, cap, rows_dev, *refs),
        out_shape=(
            jax.ShapeDtypeStruct((chips, 2 * cap + IDS, LANES), BF),
            jax.ShapeDtypeStruct((chips, 2 * cap + IDS, LANES), BF),
            jax.ShapeDtypeStruct((IDS, LANES), BF),
        ),
        in_specs=[ANY, ANY, ANY, ANY],
        out_specs=(VMEM, VMEM, VMEM),
        scratch_shapes=[
            pltpu.SMEM((features,), jnp.int32),
            pltpu.VMEM((features * pool, samples), jnp.int32),
            pltpu.VMEM((features * pool, samples), jnp.int32),
            pltpu.VMEM((samples * features, embed), BF),
            pltpu.SemaphoreType.DMA((4,)),
        ],
        compiler_params=ALL_VMEM,
        name="pack",
    )(feature_table, owner, local, pooled_grad.reshape(samples * features, embed))
    got = lax.ppermute(other, "core", [(0, 1), (1, 0)])
    for step in STEPS:
        to = [(i + 1) % chips if step == "next" else i ^ 1 for i in range(chips)]
        turn = lax.ppermute(turn, ("yx", "core"), [(2 * i, 2 * to[i]) for i in range(chips)])
    placed = pl.pallas_call(
        place_kernel,
        out_shape=jax.ShapeDtypeStruct(own.shape, BF),
        in_specs=[VMEM],
        out_specs=VMEM,
        compiler_params=PARAMS,
        name="place",
    )(own)
    send = pl.pallas_call(
        merge_kernel,
        out_shape=jax.ShapeDtypeStruct((chips, 4 * cap + IDS, LANES), BF),
        in_specs=[VMEM, VMEM, VMEM],
        out_specs=VMEM,
        scratch_shapes=[pltpu.SemaphoreType.DMA],
        compiler_params=PARAMS,
        name="merge",
    )(placed, got, turn)
    received = lax.all_to_all(send, "yx", split_axis=0, concat_axis=0, tiled=True)
    updated = pl.pallas_call(
        lambda *refs: update_kernel(cap, replicas, *refs),
        out_shape=jax.ShapeDtypeStruct((replicas, part + 2 * replicas, embed), BF),
        in_specs=[VMEM, VMEM, VMEM],
        out_specs=VMEM,
        compiler_params=PARAMS,
        name="update",
    )(received, table_rows.reshape(slots, embed), adagrad_state.reshape(slots // LANES, LANES))
    mine = lax.all_to_all(updated, "rep", split_axis=0, concat_axis=0, tiled=True)
    copies, state = pl.pallas_call(
        average_kernel,
        out_shape=(
            jax.ShapeDtypeStruct((replicas, part, embed), BF),
            jax.ShapeDtypeStruct((tables, rows_dev), F32),
        ),
        in_specs=[VMEM],
        out_specs=(VMEM, VMEM),
        compiler_params=PARAMS,
        name="average",
    )(mine)
    full = lax.all_to_all(copies, "rep", split_axis=0, concat_axis=0, tiled=True)
    return full.reshape(tables, rows_dev, embed), state


def solution(mesh):
    replicas, owners = mesh.devices.shape
    cores = mesh.devices.reshape(replicas, owners // 2, 2)
    by_core = jax.sharding.Mesh(cores, ("rep", "yx", "core"))
    every, mine = ("rep", "yx", "core"), ("yx", "core")
    placed = (
        P(every, None, None),
        P(every, None, None, None),
        P(every, None, None),
        P(),
        P(None, mine, None),
        P(None, mine),
    )
    return jax.shard_map(
        shards_fn,
        mesh=by_core,
        in_specs=placed,
        out_specs=(P(None, mine, None), P(None, mine)),
        check_vma=False,
    )
```

```python
import jax
import jax.numpy as jnp
from jax import lax
from jax.experimental import pallas as pl
from jax.experimental.pallas import tpu as pltpu
from jax.sharding import PartitionSpec as P

BF = jnp.bfloat16
F32 = jnp.float32
LANES = 128
STEPS = ("next", "next")
IDS = 8


def iota(shape, dim):
    return lax.broadcasted_iota(jnp.int32, shape, dim)


def hot16(index, *rows):
    found = index == rows[0]
    for row in rows[1:]:
        found = found | (index == row)
    return jnp.where(found, jnp.ones((), BF), jnp.zeros((), BF))


def pack_kernel(owners, cap, rows_dev, tables_hbm, owner_hbm, local_hbm, grad_hbm, own_ref,
                other_ref, turn_ref, tables_ref, owner_ref, local_ref, grad_ref, sems):
    chips = owners // 2
    pairs = (
        (owner_hbm, owner_ref),
        (tables_hbm, tables_ref),
        (local_hbm, local_ref),
        (grad_hbm, grad_ref),
    )
    copies = [pltpu.make_async_copy(a, b, sems.at[i]) for i, (a, b) in enumerate(pairs)]
    for copy in copies:
        copy.start()
    lists, samples = owner_ref.shape
    features = tables_ref.shape[0]
    pool = lists // features
    count = grad_ref.shape[0]
    copies[0].wait()
    owner = owner_ref[...]
    core = lax.axis_index("core")
    owner = owner // 2 + chips * ((owner + core) % 2)

    low = iota((samples, 2 * samples), 0)
    col = iota((samples, 2 * samples), 1)
    tri = jnp.where((low <= col), 1.0, 0.0).astype(BF)
    hot = [iota((owners, samples), 0) == owner[r : r + 1, :] for r in range(lists)]
    stacked = jnp.concatenate([jnp.where(h, 1.0, 0.0) for h in hot], axis=0).astype(BF)
    counts = jnp.dot(stacked, tri, preferred_element_type=F32)
    carry = jnp.zeros((owners, samples), F32)
    places = []
    for r in range(lists):
        block = counts[r * owners : (r + 1) * owners]
        running = block[:, :samples] + carry
        places.append(jnp.sum(jnp.where(hot[r], running, 0.0), axis=0, keepdims=True) - 1.0)
        carry = carry + block[:, samples:]
    place = jnp.concatenate(places, axis=0)

    spread = (iota((samples, count), 1) // features == iota((samples, count), 0))
    spread = jnp.where(spread, 1.0, 0.0).astype(BF)
    both = jnp.concatenate([owner.astype(F32), place], axis=0).astype(BF)
    wide = jnp.dot(both, spread, preferred_element_type=F32)
    slots = []
    lane_f = iota((lists, count), 1) % features
    slot = wide[:lists] * cap + wide[lists:]
    for p in range(pool):
        keep = iota((lists, count), 0) == lane_f * pool + p
        one = jnp.sum(jnp.where(keep, slot, 0.0), axis=0, keepdims=True)
        slots.append(jnp.broadcast_to(one, (16, count)).astype(jnp.int32).astype(jnp.int16)[0:1])

    group = 8
    rows = group * cap
    index = iota((rows, count), 0).astype(jnp.int16)
    copies[3].wait()
    grad = grad_ref[...]
    for g in range(owners // group):
        chosen = hot16(index, *[s - jnp.int16(g * rows) for s in slots])
        picked = jnp.dot(chosen, grad, preferred_element_type=F32)
        picked = picked.astype(BF)
        for k in range(group):
            part = picked[k * cap : (k + 1) * cap]
            out_ref, at = (own_ref, other_ref)[(g * group + k) // chips], (g * group + k) % chips
            out_ref[at, 0:cap, :] = part[:, :LANES]
            out_ref[at, cap : 2 * cap, :] = part[:, LANES:]

    copies[1].wait()
    copies[2].wait()
    table = jnp.zeros((lists, samples), jnp.int32)
    for f in range(features):
        table = jnp.where(iota((lists, samples), 0) // pool == f, tables_ref[f], table)
    target = table * rows_dev + local_ref[...]
    shift = ((lax.axis_index("yx") % 4) * 2 + core) * cap
    lane = place.astype(jnp.int32) + shift
    chunk = lane // LANES
    low_id = (target % 64).astype(F32)
    high_id = (target // 64).astype(F32)
    left, right = [], []
    kind = iota((IDS, samples), 0)
    for r in range(lists):
        row = slice(r, r + 1)
        value = jnp.where(kind < 3, low_id[row], high_id[row])
        value = jnp.where((kind % 3 == chunk[row]) & (kind < 6), value, 0.0)
        blocks = [jnp.where(owner[row] == o, value, 0.0) for o in range(owners)]
        left.append(jnp.concatenate(blocks, axis=0).astype(BF))
        right.append(jnp.where(lane[row] % LANES == iota((LANES, samples), 0), 1.0, 0.0).astype(BF))
    ids = lax.dot_general(
        jnp.concatenate(left, axis=1),
        jnp.concatenate(right, axis=1),
        (((1,), (1,)), ((), ())),
        preferred_element_type=F32,
    )
    ids = ids.reshape(owners, IDS, LANES).astype(BF)
    own_ref[:, 2 * cap : 2 * cap + IDS, :] = ids[:chips]
    other_ref[:, 2 * cap : 2 * cap + IDS, :] = ids[chips:]
    turn_ref[...] = jnp.zeros((IDS, LANES), BF)


def place_kernel(own_ref, out_ref):
    out_ref[...] = own_ref[...]


def merge_kernel(own_ref, got_ref, turn_ref, out_ref, sem):
    rows = own_ref.shape[1] - IDS
    core = lax.axis_index("core")

    def merge(own_at, got_at):
        came = got_ref.at[:, pl.ds(0, rows), :]
        copy = pltpu.make_async_copy(came, out_ref.at[:, pl.ds(got_at, rows), :], sem)
        copy.start()
        out_ref[:, own_at : own_at + rows, :] = own_ref[:, 0:rows, :]
        ids = own_ref[:, rows:, :].astype(F32) + got_ref[:, rows:, :].astype(F32)
        out_ref[:, 2 * rows :, :] = ids.astype(BF)
        turn = jnp.where(iota((IDS, LANES), 0) < 6, ids[0], turn_ref[...].astype(F32))
        out_ref[0, 2 * rows :, :] = turn.astype(BF)
        copy.wait()

    @pl.when(core == 0)
    def _():
        merge(0, rows)

    @pl.when(core == 1)
    def _():
        merge(rows, 0)


def update_kernel(cap, shards, recv_ref, table_ref, state_ref, out_ref):
    chips = recv_ref.shape[0]
    senders = 2 * chips
    rows = table_ref.shape[0]
    part = rows // shards
    ids = recv_ref[:, 4 * cap : 4 * cap + IDS, :].astype(F32)
    ids = jnp.sum(ids.reshape(chips // 4, 4, IDS, LANES), axis=1)
    group = 16
    where, data = [], []
    for g in range(senders // group):
        lanes = []
        for h in range(group // 8):
            x = ids[g * (group // 8) + h]
            lanes += [x[j : j + 1] + 64.0 * x[j + 3 : j + 4] for j in range(3)]
        one = jnp.concatenate(lanes, axis=1)
        one = jnp.broadcast_to(one, (16, group * cap)).astype(jnp.int32).astype(jnp.int16)
        where.append(one[0:1])
        block = recv_ref[g * group // 2 : (g + 1) * group // 2, 0 : 4 * cap, :]
        block = block.reshape(group, 2 * cap, LANES)
        halves = [
            block[:, h * cap : (h + 1) * cap, :].reshape(group * cap, LANES) for h in range(2)
        ]
        data.append(jnp.concatenate(halves, axis=1))
    state = jnp.transpose(state_ref[...])
    index = iota((part, group * cap), 0).astype(jnp.int16)
    spread = []
    for k in range(shards):
        total = jnp.zeros((part, 2 * LANES), F32)
        for g in range(senders // group):
            hot = hot16(index, where[g] - jnp.int16(k * part))
            total = total + jnp.dot(hot, data[g], preferred_element_type=F32)
        square = jnp.sum(total * total, axis=1, keepdims=True) * (1.0 / (2 * LANES))
        columns = []
        for b in range(part // LANES):
            at = k * (part // LANES) + b
            columns.append(state[:, at : at + 1] + square[b * LANES : (b + 1) * LANES])
        new = jnp.concatenate(columns, axis=0)
        old = table_ref[k * part : (k + 1) * part, :].astype(F32)
        out_ref[k, 0:part, :] = (old - 0.3 * total / jnp.sqrt(new)).astype(BF)
        wide = [jnp.transpose(jnp.broadcast_to(c, (LANES, LANES)))[0:1] for c in columns]
        spread.append(jnp.concatenate(wide, axis=1))
    whole = jnp.concatenate(spread, axis=0)
    high = whole.astype(BF).astype(F32)
    both = jnp.concatenate([high, whole - high], axis=0).astype(BF)
    for k in range(shards):
        out_ref[k, part : part + 2 * shards, :] = both


def average_kernel(got_ref, out_ref, state_ref):
    replicas, rows, embed = got_ref.shape
    part = rows - 2 * replicas
    total = got_ref[0].astype(F32)
    for r in range(1, replicas):
        total = total + got_ref[r].astype(F32)
    total = total * (1.0 / replicas)
    table = total[:part].astype(BF)
    for r in range(replicas):
        out_ref[r, :, :] = table
    state = total[part : part + replicas] + total[part + replicas :]
    wide = state_ref.shape[1] // embed
    for k in range(replicas):
        at = (k % wide) * embed
        state_ref[k // wide : k // wide + 1, at : at + embed] = state[k : k + 1]


ALL_VMEM = pltpu.CompilerParams(vmem_limit_bytes=60 * 2**20)
PARAMS = pltpu.CompilerParams(vmem_limit_bytes=32 * 2**20)
VMEM = pl.BlockSpec(memory_space=pltpu.VMEM)
ANY = pl.BlockSpec(memory_space=pl.ANY)


def shards_fn(pooled_grad, owner_ids, local_ids, feature_table, table_rows, adagrad_state):
    samples, features, embed = pooled_grad.shape
    pool = local_ids.shape[2]
    tables, rows_dev = adagrad_state.shape
    chips = lax.axis_size("yx")
    owners = 2 * chips
    replicas = lax.axis_size("rep")
    slots = tables * rows_dev
    count = samples * features * pool
    cap = 3 * count // (2 * owners)
    part = slots // replicas
    owner = jnp.transpose(owner_ids[..., 0], (1, 2, 0)).reshape(features * pool, samples)
    local = jnp.transpose(local_ids, (1, 2, 0)).reshape(features * pool, samples)
    own, other, turn = pl.pallas_call(
        lambda *refs: pack_kernel(owners, cap, rows_dev, *refs),
        out_shape=(
            jax.ShapeDtypeStruct((chips, 2 * cap + IDS, LANES), BF),
            jax.ShapeDtypeStruct((chips, 2 * cap + IDS, LANES), BF),
            jax.ShapeDtypeStruct((IDS, LANES), BF),
        ),
        in_specs=[ANY, ANY, ANY, ANY],
        out_specs=(VMEM, VMEM, VMEM),
        scratch_shapes=[
            pltpu.SMEM((features,), jnp.int32),
            pltpu.VMEM((features * pool, samples), jnp.int32),
            pltpu.VMEM((features * pool, samples), jnp.int32),
            pltpu.VMEM((samples * features, embed), BF),
            pltpu.SemaphoreType.DMA((4,)),
        ],
        compiler_params=ALL_VMEM,
        name="pack",
    )(feature_table, owner, local, pooled_grad.reshape(samples * features, embed))
    got = lax.ppermute(other, "core", [(0, 1), (1, 0)])
    for step in STEPS:
        to = [(i + 1) % chips if step == "next" else i ^ 1 for i in range(chips)]
        turn = lax.ppermute(turn, ("yx", "core"), [(2 * i, 2 * to[i]) for i in range(chips)])
    placed = pl.pallas_call(
        place_kernel,
        out_shape=jax.ShapeDtypeStruct(own.shape, BF),
        in_specs=[VMEM],
        out_specs=VMEM,
        compiler_params=PARAMS,
        name="place",
    )(own)
    send = pl.pallas_call(
        merge_kernel,
        out_shape=jax.ShapeDtypeStruct((chips, 4 * cap + IDS, LANES), BF),
        in_specs=[VMEM, VMEM, VMEM],
        out_specs=VMEM,
        scratch_shapes=[pltpu.SemaphoreType.DMA],
        compiler_params=PARAMS,
        name="merge",
    )(placed, got, turn)
    received = lax.all_to_all(send, "yx", split_axis=0, concat_axis=0, tiled=True)
    updated = pl.pallas_call(
        lambda *refs: update_kernel(cap, replicas, *refs),
        out_shape=jax.ShapeDtypeStruct((replicas, part + 2 * replicas, embed), BF),
        in_specs=[VMEM, VMEM, VMEM],
        out_specs=VMEM,
        compiler_params=PARAMS,
        name="update",
    )(received, table_rows.reshape(slots, embed), adagrad_state.reshape(slots // LANES, LANES))
    mine = lax.all_to_all(updated, "rep", split_axis=0, concat_axis=0, tiled=True)
    copies, state = pl.pallas_call(
        average_kernel,
        out_shape=(
            jax.ShapeDtypeStruct((replicas, part, embed), BF),
            jax.ShapeDtypeStruct((tables, rows_dev), F32),
        ),
        in_specs=[VMEM],
        out_specs=(VMEM, VMEM),
        compiler_params=PARAMS,
        name="average",
    )(mine)
    full = lax.all_to_all(copies, "rep", split_axis=0, concat_axis=0, tiled=True)
    return full.reshape(tables, rows_dev, embed), state


def solution(mesh):
    replicas, owners = mesh.devices.shape
    cores = mesh.devices.reshape(replicas, owners // 2, 2)
    by_core = jax.sharding.Mesh(cores, ("rep", "yx", "core"))
    every, mine = ("rep", "yx", "core"), ("yx", "core")
    placed = (
        P(every, None, None),
        P(every, None, None, None),
        P(every, None, None),
        P(),
        P(None, mine, None),
        P(None, mine),
    )
    return jax.shard_map(
        shards_fn,
        mesh=by_core,
        in_specs=placed,
        out_specs=(P(None, mine, None), P(None, mine)),
        check_vma=False,
    )
```

```python
import jax
import jax.numpy as jnp
from jax import lax
from jax.experimental import pallas as pl
from jax.experimental.pallas import tpu as pltpu
from jax.sharding import PartitionSpec as P

BF = jnp.bfloat16
F32 = jnp.float32
LANES = 128
STEPS = ("next", "near")
IDS = 8


def iota(shape, dim):
    return lax.broadcasted_iota(jnp.int32, shape, dim)


def hot16(index, *rows):
    found = index == rows[0]
    for row in rows[1:]:
        found = found | (index == row)
    return jnp.where(found, jnp.ones((), BF), jnp.zeros((), BF))


def pack_kernel(owners, cap, rows_dev, tables_hbm, owner_hbm, local_hbm, grad_hbm, own_ref,
                other_ref, turn_ref, tables_ref, owner_ref, local_ref, grad_ref, sems):
    chips = owners // 2
    pairs = (
        (owner_hbm, owner_ref),
        (tables_hbm, tables_ref),
        (local_hbm, local_ref),
        (grad_hbm, grad_ref),
    )
    copies = [pltpu.make_async_copy(a, b, sems.at[i]) for i, (a, b) in enumerate(pairs)]
    for copy in copies:
        copy.start()
    lists, samples = owner_ref.shape
    features = tables_ref.shape[0]
    pool = lists // features
    count = grad_ref.shape[0]
    copies[0].wait()
    owner = owner_ref[...]
    core = lax.axis_index("core")
    owner = owner // 2 + chips * ((owner + core) % 2)

    low = iota((samples, 2 * samples), 0)
    col = iota((samples, 2 * samples), 1)
    tri = jnp.where((low <= col), 1.0, 0.0).astype(BF)
    hot = [iota((owners, samples), 0) == owner[r : r + 1, :] for r in range(lists)]
    stacked = jnp.concatenate([jnp.where(h, 1.0, 0.0) for h in hot], axis=0).astype(BF)
    counts = jnp.dot(stacked, tri, preferred_element_type=F32)
    carry = jnp.zeros((owners, samples), F32)
    places = []
    for r in range(lists):
        block = counts[r * owners : (r + 1) * owners]
        running = block[:, :samples] + carry
        places.append(jnp.sum(jnp.where(hot[r], running, 0.0), axis=0, keepdims=True) - 1.0)
        carry = carry + block[:, samples:]
    place = jnp.concatenate(places, axis=0)

    spread = (iota((samples, count), 1) // features == iota((samples, count), 0))
    spread = jnp.where(spread, 1.0, 0.0).astype(BF)
    both = jnp.concatenate([owner.astype(F32), place], axis=0).astype(BF)
    wide = jnp.dot(both, spread, preferred_element_type=F32)
    slots = []
    lane_f = iota((lists, count), 1) % features
    slot = wide[:lists] * cap + wide[lists:]
    for p in range(pool):
        keep = iota((lists, count), 0) == lane_f * pool + p
        one = jnp.sum(jnp.where(keep, slot, 0.0), axis=0, keepdims=True)
        slots.append(jnp.broadcast_to(one, (16, count)).astype(jnp.int32).astype(jnp.int16)[0:1])

    group = 8
    rows = group * cap
    index = iota((rows, count), 0).astype(jnp.int16)
    copies[3].wait()
    grad = grad_ref[...]
    for g in range(owners // group):
        chosen = hot16(index, *[s - jnp.int16(g * rows) for s in slots])
        picked = jnp.dot(chosen, grad, preferred_element_type=F32)
        picked = picked.astype(BF)
        for k in range(group):
            part = picked[k * cap : (k + 1) * cap]
            out_ref, at = (own_ref, other_ref)[(g * group + k) // chips], (g * group + k) % chips
            out_ref[at, 0:cap, :] = part[:, :LANES]
            out_ref[at, cap : 2 * cap, :] = part[:, LANES:]

    copies[1].wait()
    copies[2].wait()
    table = jnp.zeros((lists, samples), jnp.int32)
    for f in range(features):
        table = jnp.where(iota((lists, samples), 0) // pool == f, tables_ref[f], table)
    target = table * rows_dev + local_ref[...]
    shift = ((lax.axis_index("yx") % 4) * 2 + core) * cap
    lane = place.astype(jnp.int32) + shift
    chunk = lane // LANES
    low_id = (target % 64).astype(F32)
    high_id = (target // 64).astype(F32)
    left, right = [], []
    kind = iota((IDS, samples), 0)
    for r in range(lists):
        row = slice(r, r + 1)
        value = jnp.where(kind < 3, low_id[row], high_id[row])
        value = jnp.where((kind % 3 == chunk[row]) & (kind < 6), value, 0.0)
        blocks = [jnp.where(owner[row] == o, value, 0.0) for o in range(owners)]
        left.append(jnp.concatenate(blocks, axis=0).astype(BF))
        right.append(jnp.where(lane[row] % LANES == iota((LANES, samples), 0), 1.0, 0.0).astype(BF))
    ids = lax.dot_general(
        jnp.concatenate(left, axis=1),
        jnp.concatenate(right, axis=1),
        (((1,), (1,)), ((), ())),
        preferred_element_type=F32,
    )
    ids = ids.reshape(owners, IDS, LANES).astype(BF)
    own_ref[:, 2 * cap : 2 * cap + IDS, :] = ids[:chips]
    other_ref[:, 2 * cap : 2 * cap + IDS, :] = ids[chips:]
    turn_ref[...] = jnp.zeros((IDS, LANES), BF)


def place_kernel(own_ref, out_ref):
    out_ref[...] = own_ref[...]


def merge_kernel(own_ref, got_ref, turn_ref, out_ref, sem):
    rows = own_ref.shape[1] - IDS
    core = lax.axis_index("core")

    def merge(own_at, got_at):
        came = got_ref.at[:, pl.ds(0, rows), :]
        copy = pltpu.make_async_copy(came, out_ref.at[:, pl.ds(got_at, rows), :], sem)
        copy.start()
        out_ref[:, own_at : own_at + rows, :] = own_ref[:, 0:rows, :]
        ids = own_ref[:, rows:, :].astype(F32) + got_ref[:, rows:, :].astype(F32)
        out_ref[:, 2 * rows :, :] = ids.astype(BF)
        turn = jnp.where(iota((IDS, LANES), 0) < 6, ids[0], turn_ref[...].astype(F32))
        out_ref[0, 2 * rows :, :] = turn.astype(BF)
        copy.wait()

    @pl.when(core == 0)
    def _():
        merge(0, rows)

    @pl.when(core == 1)
    def _():
        merge(rows, 0)


def update_kernel(cap, shards, recv_ref, table_ref, state_ref, out_ref):
    chips = recv_ref.shape[0]
    senders = 2 * chips
    rows = table_ref.shape[0]
    part = rows // shards
    ids = recv_ref[:, 4 * cap : 4 * cap + IDS, :].astype(F32)
    ids = jnp.sum(ids.reshape(chips // 4, 4, IDS, LANES), axis=1)
    group = 16
    where, data = [], []
    for g in range(senders // group):
        lanes = []
        for h in range(group // 8):
            x = ids[g * (group // 8) + h]
            lanes += [x[j : j + 1] + 64.0 * x[j + 3 : j + 4] for j in range(3)]
        one = jnp.concatenate(lanes, axis=1)
        one = jnp.broadcast_to(one, (16, group * cap)).astype(jnp.int32).astype(jnp.int16)
        where.append(one[0:1])
        block = recv_ref[g * group // 2 : (g + 1) * group // 2, 0 : 4 * cap, :]
        block = block.reshape(group, 2 * cap, LANES)
        halves = [
            block[:, h * cap : (h + 1) * cap, :].reshape(group * cap, LANES) for h in range(2)
        ]
        data.append(jnp.concatenate(halves, axis=1))
    state = jnp.transpose(state_ref[...])
    index = iota((part, group * cap), 0).astype(jnp.int16)
    spread = []
    for k in range(shards):
        total = jnp.zeros((part, 2 * LANES), F32)
        for g in range(senders // group):
            hot = hot16(index, where[g] - jnp.int16(k * part))
            total = total + jnp.dot(hot, data[g], preferred_element_type=F32)
        square = jnp.sum(total * total, axis=1, keepdims=True) * (1.0 / (2 * LANES))
        columns = []
        for b in range(part // LANES):
            at = k * (part // LANES) + b
            columns.append(state[:, at : at + 1] + square[b * LANES : (b + 1) * LANES])
        new = jnp.concatenate(columns, axis=0)
        old = table_ref[k * part : (k + 1) * part, :].astype(F32)
        out_ref[k, 0:part, :] = (old - 0.3 * total / jnp.sqrt(new)).astype(BF)
        wide = [jnp.transpose(jnp.broadcast_to(c, (LANES, LANES)))[0:1] for c in columns]
        spread.append(jnp.concatenate(wide, axis=1))
    whole = jnp.concatenate(spread, axis=0)
    high = whole.astype(BF).astype(F32)
    both = jnp.concatenate([high, whole - high], axis=0).astype(BF)
    for k in range(shards):
        out_ref[k, part : part + 2 * shards, :] = both


def average_kernel(got_ref, out_ref, state_ref):
    replicas, rows, embed = got_ref.shape
    part = rows - 2 * replicas
    total = got_ref[0].astype(F32)
    for r in range(1, replicas):
        total = total + got_ref[r].astype(F32)
    total = total * (1.0 / replicas)
    table = total[:part].astype(BF)
    for r in range(replicas):
        out_ref[r, :, :] = table
    state = total[part : part + replicas] + total[part + replicas :]
    wide = state_ref.shape[1] // embed
    for k in range(replicas):
        at = (k % wide) * embed
        state_ref[k // wide : k // wide + 1, at : at + embed] = state[k : k + 1]


ALL_VMEM = pltpu.CompilerParams(vmem_limit_bytes=60 * 2**20)
PARAMS = pltpu.CompilerParams(vmem_limit_bytes=32 * 2**20)
VMEM = pl.BlockSpec(memory_space=pltpu.VMEM)
ANY = pl.BlockSpec(memory_space=pl.ANY)


def shards_fn(pooled_grad, owner_ids, local_ids, feature_table, table_rows, adagrad_state):
    samples, features, embed = pooled_grad.shape
    pool = local_ids.shape[2]
    tables, rows_dev = adagrad_state.shape
    chips = lax.axis_size("yx")
    owners = 2 * chips
    replicas = lax.axis_size("rep")
    slots = tables * rows_dev
    count = samples * features * pool
    cap = 3 * count // (2 * owners)
    part = slots // replicas
    owner = jnp.transpose(owner_ids[..., 0], (1, 2, 0)).reshape(features * pool, samples)
    local = jnp.transpose(local_ids, (1, 2, 0)).reshape(features * pool, samples)
    own, other, turn = pl.pallas_call(
        lambda *refs: pack_kernel(owners, cap, rows_dev, *refs),
        out_shape=(
            jax.ShapeDtypeStruct((chips, 2 * cap + IDS, LANES), BF),
            jax.ShapeDtypeStruct((chips, 2 * cap + IDS, LANES), BF),
            jax.ShapeDtypeStruct((IDS, LANES), BF),
        ),
        in_specs=[ANY, ANY, ANY, ANY],
        out_specs=(VMEM, VMEM, VMEM),
        scratch_shapes=[
            pltpu.SMEM((features,), jnp.int32),
            pltpu.VMEM((features * pool, samples), jnp.int32),
            pltpu.VMEM((features * pool, samples), jnp.int32),
            pltpu.VMEM((samples * features, embed), BF),
            pltpu.SemaphoreType.DMA((4,)),
        ],
        compiler_params=ALL_VMEM,
        name="pack",
    )(feature_table, owner, local, pooled_grad.reshape(samples * features, embed))
    got = lax.ppermute(other, "core", [(0, 1), (1, 0)])
    for step in STEPS:
        to = [(i + 1) % chips if step == "next" else i ^ 1 for i in range(chips)]
        turn = lax.ppermute(turn, ("yx", "core"), [(2 * i, 2 * to[i]) for i in range(chips)])
    placed = pl.pallas_call(
        place_kernel,
        out_shape=jax.ShapeDtypeStruct(own.shape, BF),
        in_specs=[VMEM],
        out_specs=VMEM,
        compiler_params=PARAMS,
        name="place",
    )(own)
    send = pl.pallas_call(
        merge_kernel,
        out_shape=jax.ShapeDtypeStruct((chips, 4 * cap + IDS, LANES), BF),
        in_specs=[VMEM, VMEM, VMEM],
        out_specs=VMEM,
        scratch_shapes=[pltpu.SemaphoreType.DMA],
        compiler_params=PARAMS,
        name="merge",
    )(placed, got, turn)
    received = lax.all_to_all(send, "yx", split_axis=0, concat_axis=0, tiled=True)
    updated = pl.pallas_call(
        lambda *refs: update_kernel(cap, replicas, *refs),
        out_shape=jax.ShapeDtypeStruct((replicas, part + 2 * replicas, embed), BF),
        in_specs=[VMEM, VMEM, VMEM],
        out_specs=VMEM,
        compiler_params=PARAMS,
        name="update",
    )(received, table_rows.reshape(slots, embed), adagrad_state.reshape(slots // LANES, LANES))
    mine = lax.all_to_all(updated, "rep", split_axis=0, concat_axis=0, tiled=True)
    copies, state = pl.pallas_call(
        average_kernel,
        out_shape=(
            jax.ShapeDtypeStruct((replicas, part, embed), BF),
            jax.ShapeDtypeStruct((tables, rows_dev), F32),
        ),
        in_specs=[VMEM],
        out_specs=(VMEM, VMEM),
        compiler_params=PARAMS,
        name="average",
    )(mine)
    full = lax.all_to_all(copies, "rep", split_axis=0, concat_axis=0, tiled=True)
    return full.reshape(tables, rows_dev, embed), state


def solution(mesh):
    replicas, owners = mesh.devices.shape
    cores = mesh.devices.reshape(replicas, owners // 2, 2)
    by_core = jax.sharding.Mesh(cores, ("rep", "yx", "core"))
    every, mine = ("rep", "yx", "core"), ("yx", "core")
    placed = (
        P(every, None, None),
        P(every, None, None, None),
        P(every, None, None),
        P(),
        P(None, mine, None),
        P(None, mine),
    )
    return jax.shard_map(
        shards_fn,
        mesh=by_core,
        in_specs=placed,
        out_specs=(P(None, mine, None), P(None, mine)),
        check_vma=False,
    )
```
